32 devices in a mesh: groups: 2 (over x), blk: 16 (over z, y, core).
Axes of the slice: x: 2, y: 2, z: 4, core: 2. Of those that a mesh axis runs over, the one named last changes fastest.
Arguments:
- frames: bfloat16 [256, 16384], P(('groups', 'blk')), parts along dimension 0
- basis: bfloat16 [256, 64], P(('groups', 'blk')), parts along dimension 0, may hold values from -6 to 6
- density: bfloat16 [256], P(('groups', 'blk')), parts along dimension 0, may hold values from 0.25 to 4
Outputs:
- residual_block: bfloat16 [256, 64], P(('groups', 'blk')), parts along dimension 0
- coefficients: float32 [128, 64], P('groups'), parts along dimension 0
The draws below stay inside these ranges and needn't reach their ends.
There are 2 independent parts, one for each index of `groups`. The reference program is written for one: setup_inputs(seed, part) draws one part's arguments, and reference() takes and returns one part's arrays. A program takes and returns all parts, laid end to end along the dimension named above; each array names one. Nothing has to cross between parts.
All inputs are finite; a program needn't handle non-finite values.
Results may differ from the reference program's by a relative error of at most 0.0045.
Values may be sent and summed in bfloat16 or wider, within the bound.
A program may use at most 64 MiB of HBM per device.

```python
import math
import jax
import jax.numpy as jnp
from jax import lax

F = 16384
BASIS = 64
ROWS = 8
FRAMES = 128
N_BLK = 16


def draw_frames(key, part):
    key_time = jax.random.fold_in(key, 21)
    key_freq = jax.random.fold_in(key, 22)
    key_phase = jax.random.fold_in(key, 23)
    key_jitter = jax.random.fold_in(key, 24)
    span = FRAMES / 16.0
    amplitude = math.sqrt(6.0)
    times = jax.random.uniform(key_time, (FRAMES, 1), jnp.float32, 0.0, span)
    spread = jax.random.uniform(key_freq, (1, F), jnp.float32, -0.49, 0.49)
    omega = jnp.tan(math.pi * spread)
    phase = jax.random.uniform(key_phase, (1, F), jnp.float32, -math.pi, math.pi)
    jitter = 0.25 * jax.random.normal(key_jitter, (FRAMES, F), jnp.float32)
    features = amplitude * jnp.cos(times * omega + phase) + jitter
    return features.astype(jnp.bfloat16)


def shard_levels(stream_key, dims, pieces, low, top_value):
    factor_of, own = 1.0, jax.random.fold_in(stream_key, 6)
    for dim, parts in pieces:
        steps = jnp.exp(jax.random.uniform(jax.random.fold_in(own, dim), (parts,), jnp.float32, low / len(pieces), top_value / len(pieces)))
        factor_of = factor_of * jnp.repeat(steps, dims[dim] // parts).reshape([-1 if axis == dim else 1 for axis in range(len(dims))])
    return factor_of


def bell_draw(own_key, shape, scale, limit, cuts=(), held_as=jnp.bfloat16):
    entries = scale * jax.random.normal(own_key, shape, jnp.float32)
    if cuts:
        entries = entries * shard_levels(own_key, shape, cuts, -0.22, 0.18)
    return jnp.clip(entries, -limit, limit).astype(held_as)


def setup_inputs(seed: int = 0, part: int = 0) -> dict:
    arg_keys = jax.random.split(jax.random.key(seed), 4)
    part_splits = jax.random.split(jax.random.fold_in(arg_keys[3], part), 4)
    return {
        "frames": draw_frames(jax.random.fold_in(jax.random.fold_in(arg_keys[3], part), 71), part),
        "basis": bell_draw(part_splits[1], (FRAMES, BASIS), 1.0, 6.0, ((0, 16),)),
        "density": jnp.clip(jnp.exp(math.log(4.0) - 2.7725887 * jax.random.uniform(part_splits[2], (FRAMES,), jnp.float32) ** shard_levels(part_splits[2], (FRAMES,), ((0, 16),), -0.2, 0.2)), 0.25, 4.0).astype(jnp.bfloat16),
    }


def reference(frames, basis, density):
    norms = jnp.sum(jnp.square(frames.astype(jnp.float32)), axis=1)
    density_f = density.astype(jnp.float32)

    def one_block(block_index):
        block_rows = lax.dynamic_slice_in_dim(frames, block_index * ROWS, ROWS, 0)
        block_norms = lax.dynamic_slice_in_dim(norms, block_index * ROWS, ROWS, 0)
        inner_products = lax.dot_general(block_rows, frames, (((1,), (1,)), ((), ())), preferred_element_type=jnp.float32)
        squared_dist = block_norms[:, None] + norms[None, :] - 2.0 * inner_products
        weight = (jnp.exp(-squared_dist / F) * density_f[None, :]).astype(jnp.bfloat16)
        numer = jnp.dot(weight, basis, preferred_element_type=jnp.float32)
        totals = jnp.sum(weight.astype(jnp.float32), axis=1)
        return numer / totals[:, None]

    applied = lax.map(one_block, jnp.arange(N_BLK, dtype=jnp.int32)).reshape(FRAMES, BASIS)
    basis_f = basis.astype(jnp.float32)
    coefficients = lax.dot_general(basis_f, applied, (((0,), (0,)), ((), ())), precision=lax.Precision.HIGHEST, preferred_element_type=jnp.float32)
    projection = jnp.dot(basis_f, coefficients, precision=lax.Precision.HIGHEST, preferred_element_type=jnp.float32)
    residual_block = (applied - projection / FRAMES).astype(jnp.bfloat16)
    return residual_block, coefficients
```

```python
import functools

import jax
import jax.numpy as jnp
from jax import lax
from jax.experimental import pallas as pl
from jax.experimental.pallas import tpu as pltpu
from jax.sharding import PartitionSpec as P

LANES = 128


def partners(me, n):
    half = n // 2
    mine = me // half
    far = [(1 - mine) * half + lax.rem(me + j, half) for j in range(half)]
    near = [mine * half + lax.rem(me + j, half) for j in range(1, half)]
    return far + near


def kernel(
    n,
    frames_ref,
    basis_ref,
    density_ref,
    residual_ref,
    coef_ref,
    gathered,
    aux,
    partial,
    arrived,
    applied,
    own_sem,
    send_sem,
    recv_sem,
):
    me = lax.axis_index("blk")
    rows, features = frames_ref.shape
    width = basis_ref.shape[1]
    span = features // n
    total = n * rows
    others = partners(me, n)

    barrier = pltpu.get_barrier_semaphore()
    for other in others:
        pl.semaphore_signal(
            barrier, inc=1, device_id={"blk": other}, device_id_type=pl.DeviceIdType.MESH
        )

    own = pltpu.make_async_copy(
        frames_ref.at[:, pl.ds(pl.multiple_of(me * span, span), span)], gathered.at[me], own_sem
    )
    own.start()

    row_id = lax.broadcasted_iota(jnp.int32, (rows, rows), 0)
    col_id = lax.broadcasted_iota(jnp.int32, (rows, rows), 1)
    density_row = density_ref[...].astype(jnp.float32)
    density_col = jnp.sum(
        jnp.where(row_id == col_id, jnp.broadcast_to(density_row, (rows, rows)), 0.0),
        axis=1,
        keepdims=True,
    )
    own_basis = basis_ref[...].astype(jnp.float32)
    own_wide = jnp.concatenate(
        [own_basis, jnp.broadcast_to(density_col, (rows, LANES - width))], axis=1
    )
    aux[me] = own_wide.astype(jnp.bfloat16)

    pl.semaphore_wait(barrier, n - 1)

    def send(src, dst, slot, other):
        pltpu.make_async_remote_copy(
            src_ref=src,
            dst_ref=dst,
            send_sem=send_sem.at[slot],
            recv_sem=recv_sem.at[slot],
            device_id={"blk": other},
            device_id_type=pl.DeviceIdType.MESH,
        ).start()

    def wait_all(buffer, sem):
        part = buffer.at[pl.ds(0, n - 1)]
        pltpu.make_async_copy(part, part, sem).wait()

    for other in others:
        send(
            frames_ref.at[:, pl.ds(pl.multiple_of(other * span, span), span)],
            gathered.at[me],
            0,
            other,
        )
    for other in others:
        send(aux.at[me], aux.at[me], 1, other)

    wait_all(aux, recv_sem.at[1])
    wide = aux[...].astype(jnp.float32).reshape(total, LANES)
    eye = lax.broadcasted_iota(jnp.int32, (total, total), 0) == lax.broadcasted_iota(
        jnp.int32, (total, total), 1
    )
    density_all = jnp.sum(jnp.where(eye, wide[:, width : width + 1], 0.0), axis=0, keepdims=True)
    lane = lax.broadcasted_iota(jnp.int32, (total, LANES), 1)
    vectors = jnp.where(lane < width, wide, 0.0)
    vectors_bf = vectors.astype(jnp.bfloat16)
    own_lane = lax.broadcasted_iota(jnp.int32, (rows, LANES), 1)
    own_vectors = jnp.where(own_lane < width, own_wide, 0.0)
    overlap = lax.dot_general(
        own_vectors.astype(jnp.bfloat16),
        vectors_bf,
        (((1,), (1,)), ((), ())),
        preferred_element_type=jnp.float32,
    )
    onto = jnp.concatenate([jnp.transpose(vectors)[:width], overlap], axis=0)

    own.wait()
    wait_all(gathered, recv_sem.at[0])
    block = gathered[...].reshape(total, span)
    gram = lax.dot_general(
        block, block, (((1,), (1,)), ((), ())), preferred_element_type=jnp.float32
    )
    diagonal = jnp.where(eye, gram, 0.0)
    dist = (
        jnp.sum(diagonal, axis=1, keepdims=True)
        + jnp.sum(diagonal, axis=0, keepdims=True)
        - 2.0 * gram
    )
    partial[...] = dist.reshape(n, rows, total)
    for other in others:
        send(partial.at[other], arrived.at[me], 2, other)
    arrived[me] = partial[me]
    wait_all(arrived, recv_sem.at[2])

    squared_dist = jnp.sum(arrived[...], axis=0)
    weight = (jnp.exp(-squared_dist / features) * density_all).astype(jnp.bfloat16)
    numer = jnp.dot(weight, vectors_bf, preferred_element_type=jnp.float32)
    totals = jnp.sum(weight.astype(jnp.float32), axis=1, keepdims=True)
    own_applied = numer / totals
    applied[me] = own_applied
    for other in others:
        send(applied.at[me], applied.at[me], 3, other)
    wait_all(applied, recv_sem.at[3])

    products = jnp.dot(
        onto,
        applied[...].reshape(total, LANES),
        precision=lax.Precision.HIGHEST,
        preferred_element_type=jnp.float32,
    )
    coef_ref[...] = products[:width, :width]
    residual = own_applied - products[width:] / total
    residual_ref[...] = residual[:, :width].astype(jnp.bfloat16)

    wait_all(gathered, send_sem.at[0])
    wait_all(aux, send_sem.at[1])
    wait_all(arrived, send_sem.at[2])
    wait_all(applied, send_sem.at[3])


def shards(n, frames, basis, density):
    rows, features = frames.shape
    width = basis.shape[1]
    total = n * rows
    vmem = pl.BlockSpec(memory_space=pltpu.VMEM)
    return pl.pallas_call(
        functools.partial(kernel, n),
        out_shape=(
            jax.ShapeDtypeStruct((rows, width), jnp.bfloat16),
            jax.ShapeDtypeStruct((width, width), jnp.float32),
        ),
        in_specs=[pl.BlockSpec(memory_space=pl.ANY), vmem, vmem],
        out_specs=(vmem, vmem),
        scratch_shapes=[
            pltpu.VMEM((n, rows, features // n), jnp.bfloat16),
            pltpu.VMEM((n, rows, LANES), jnp.bfloat16),
            pltpu.VMEM((n, rows, total), jnp.float32),
            pltpu.VMEM((n, rows, total), jnp.float32),
            pltpu.VMEM((n, rows, LANES), jnp.float32),
            pltpu.SemaphoreType.DMA,
            pltpu.SemaphoreType.DMA((4,)),
            pltpu.SemaphoreType.DMA((4,)),
        ],
        compiler_params=pltpu.CompilerParams(
            collective_id=0, has_side_effects=True, vmem_limit_bytes=32 * 1024 * 1024
        ),
        cost_estimate=pl.CostEstimate(
            flops=2 * total * total * (features // n),
            bytes_accessed=2 * rows * features,
            transcendentals=rows * total,
        ),
    )(frames, basis, density.reshape(1, rows))


def solution(mesh):
    placed = (P(("groups", "blk"), None), P(("groups", "blk"), None), P(("groups", "blk")))
    return jax.shard_map(
        functools.partial(shards, mesh.shape["blk"]),
        mesh=mesh,
        in_specs=placed,
        out_specs=(P(("groups", "blk"), None), P("groups", None)),
        check_vma=False,
    )
```

```python
import functools

import jax
import jax.numpy as jnp
from jax import lax
from jax.experimental import pallas as pl
from jax.experimental.pallas import tpu as pltpu
from jax.sharding import PartitionSpec as P

LANES = 128


def partners(me, n):
    half = n // 2
    mine = me // half
    far = [(1 - mine) * half + lax.rem(me + j, half) for j in range(half)]
    near = [mine * half + lax.rem(me + j, half) for j in range(1, half)]
    return far + near


def kernel(
    n,
    frames_ref,
    basis_ref,
    density_ref,
    residual_ref,
    coef_ref,
    gathered,
    aux,
    partial,
    arrived,
    applied,
    basis_vmem,
    density_vmem,
    own_sem,
    send_sem,
    recv_sem,
):
    me = lax.axis_index("blk")
    rows, features = frames_ref.shape
    width = basis_ref.shape[1]
    span = features // n
    total = n * rows
    others = partners(me, n)

    fetch_basis = pltpu.make_async_copy(basis_ref, basis_vmem, own_sem.at[1])
    fetch_basis.start()
    fetch_density = pltpu.make_async_copy(density_ref, density_vmem, own_sem.at[2])
    fetch_density.start()

    barrier = pltpu.get_barrier_semaphore()
    for other in others:
        pl.semaphore_signal(
            barrier, inc=1, device_id={"blk": other}, device_id_type=pl.DeviceIdType.MESH
        )

    own = pltpu.make_async_copy(
        frames_ref.at[:, pl.ds(pl.multiple_of(me * span, span), span)], gathered.at[me], own_sem.at[0]
    )
    own.start()

    row_id = lax.broadcasted_iota(jnp.int32, (rows, rows), 0)
    col_id = lax.broadcasted_iota(jnp.int32, (rows, rows), 1)
    fetch_density.wait()
    density_row = density_vmem[...].astype(jnp.float32)
    density_col = jnp.sum(
        jnp.where(row_id == col_id, jnp.broadcast_to(density_row, (rows, rows)), 0.0),
        axis=1,
        keepdims=True,
    )
    fetch_basis.wait()
    own_basis = basis_vmem[...].astype(jnp.float32)
    own_wide = jnp.concatenate(
        [own_basis, jnp.broadcast_to(density_col, (rows, LANES - width))], axis=1
    )
    aux[me] = own_wide.astype(jnp.bfloat16)

    pl.semaphore_wait(barrier, n - 1)

    def send(src, dst, slot, other):
        pltpu.make_async_remote_copy(
            src_ref=src,
            dst_ref=dst,
            send_sem=send_sem.at[slot],
            recv_sem=recv_sem.at[slot],
            device_id={"blk": other},
            device_id_type=pl.DeviceIdType.MESH,
        ).start()

    def wait_all(buffer, sem):
        part = buffer.at[pl.ds(0, n - 1)]
        pltpu.make_async_copy(part, part, sem).wait()

    for other in others:
        send(
            frames_ref.at[:, pl.ds(pl.multiple_of(other * span, span), span)],
            gathered.at[me],
            0,
            other,
        )
    for other in others:
        send(aux.at[me], aux.at[me], 1, other)

    wait_all(aux, recv_sem.at[1])
    wide = aux[...].astype(jnp.float32).reshape(total, LANES)
    eye = lax.broadcasted_iota(jnp.int32, (total, total), 0) == lax.broadcasted_iota(
        jnp.int32, (total, total), 1
    )
    density_all = jnp.sum(jnp.where(eye, wide[:, width : width + 1], 0.0), axis=0, keepdims=True)
    lane = lax.broadcasted_iota(jnp.int32, (total, LANES), 1)
    vectors = jnp.where(lane < width, wide, 0.0)
    vectors_bf = vectors.astype(jnp.bfloat16)
    own_lane = lax.broadcasted_iota(jnp.int32, (rows, LANES), 1)
    own_vectors = jnp.where(own_lane < width, own_wide, 0.0)
    overlap = lax.dot_general(
        own_vectors.astype(jnp.bfloat16),
        vectors_bf,
        (((1,), (1,)), ((), ())),
        preferred_element_type=jnp.float32,
    )
    onto = jnp.concatenate([jnp.transpose(vectors)[:width], overlap], axis=0)

    own.wait()
    wait_all(gathered, recv_sem.at[0])
    block = gathered[...].reshape(total, span)
    gram = lax.dot_general(
        block, block, (((1,), (1,)), ((), ())), preferred_element_type=jnp.float32
    )
    diagonal = jnp.where(eye, gram, 0.0)
    dist = (
        jnp.sum(diagonal, axis=1, keepdims=True)
        + jnp.sum(diagonal, axis=0, keepdims=True)
        - 2.0 * gram
    )
    partial[...] = dist.reshape(n, rows, total)
    for other in others:
        send(partial.at[other], arrived.at[me], 2, other)
    arrived[me] = partial[me]
    wait_all(arrived, recv_sem.at[2])

    squared_dist = jnp.sum(arrived[...], axis=0)
    weight = (jnp.exp(-squared_dist / features) * density_all).astype(jnp.bfloat16)
    numer = jnp.dot(weight, vectors_bf, preferred_element_type=jnp.float32)
    totals = jnp.sum(weight.astype(jnp.float32), axis=1, keepdims=True)
    own_applied = numer / totals
    applied[me] = own_applied
    for other in others:
        send(applied.at[me], applied.at[me], 3, other)
    wait_all(applied, recv_sem.at[3])

    products = jnp.dot(
        onto,
        applied[...].reshape(total, LANES),
        precision=lax.Precision.HIGHEST,
        preferred_element_type=jnp.float32,
    )
    coef_ref[...] = products[:width, :width]
    residual = own_applied - products[width:] / total
    residual_ref[...] = residual[:, :width].astype(jnp.bfloat16)

    wait_all(gathered, send_sem.at[0])
    wait_all(aux, send_sem.at[1])
    wait_all(arrived, send_sem.at[2])
    wait_all(applied, send_sem.at[3])


def shards(n, frames, basis, density):
    rows, features = frames.shape
    width = basis.shape[1]
    total = n * rows
    vmem = pl.BlockSpec(memory_space=pltpu.VMEM)
    return pl.pallas_call(
        functools.partial(kernel, n),
        out_shape=(
            jax.ShapeDtypeStruct((rows, width), jnp.bfloat16),
            jax.ShapeDtypeStruct((width, width), jnp.float32),
        ),
        in_specs=[pl.BlockSpec(memory_space=pltpu.HBM)] * 3,
        out_specs=(vmem, vmem),
        scratch_shapes=[
            pltpu.VMEM((n, rows, features // n), jnp.bfloat16),
            pltpu.VMEM((n, rows, LANES), jnp.bfloat16),
            pltpu.VMEM((n, rows, total), jnp.float32),
            pltpu.VMEM((n, rows, total), jnp.float32),
            pltpu.VMEM((n, rows, LANES), jnp.float32),
            pltpu.VMEM((rows, width), jnp.bfloat16),
            pltpu.VMEM((1, rows), jnp.bfloat16),
            pltpu.SemaphoreType.DMA((3,)),
            pltpu.SemaphoreType.DMA((4,)),
            pltpu.SemaphoreType.DMA((4,)),
        ],
        compiler_params=pltpu.CompilerParams(
            collective_id=0, has_side_effects=True, vmem_limit_bytes=64 * 1024 * 1024
        ),
        cost_estimate=pl.CostEstimate(
            flops=2 * total * total * (features // n),
            bytes_accessed=2 * rows * features,
            transcendentals=rows * total,
        ),
    )(frames, basis, density.reshape(1, rows))


def solution(mesh):
    placed = (P(("groups", "blk"), None), P(("groups", "blk"), None), P(("groups", "blk")))
    return jax.shard_map(
        functools.partial(shards, mesh.shape["blk"]),
        mesh=mesh,
        in_specs=placed,
        out_specs=(P(("groups", "blk"), None), P("groups", None)),
        check_vma=False,
    )
```

```python
import functools

import jax
import jax.numpy as jnp
from jax import lax
from jax.experimental import pallas as pl
from jax.experimental.pallas import tpu as pltpu
from jax.sharding import PartitionSpec as P

LANES = 128


def partners(me, n):
    half = n // 2
    upper = me >= half
    place = jnp.where(upper, me - half, me)
    mine = jnp.where(upper, half, 0)
    turned = [place] + [
        jnp.where(place >= half - j, place + j - half, place + j) for j in range(1, half)
    ]
    return [half - mine + t for t in turned] + [mine + t for t in turned[1:]]


def kernel(
    n,
    frames_ref,
    basis_ref,
    density_ref,
    both_ref,
    gathered,
    aux,
    partial,
    arrived,
    applied,
    basis_vmem,
    density_vmem,
    own_sem,
    send_sem,
    recv_sem,
):
    me = lax.axis_index("blk")
    rows, features = frames_ref.shape
    width = basis_ref.shape[1]
    span = features // n
    total = n * rows
    others = partners(me, n)

    fetch_basis = pltpu.make_async_copy(basis_ref, basis_vmem, own_sem.at[1])
    fetch_basis.start()
    fetch_density = pltpu.make_async_copy(density_ref, density_vmem, own_sem.at[2])
    fetch_density.start()

    barrier = pltpu.get_barrier_semaphore()
    for other in others:
        pl.semaphore_signal(
            barrier, inc=1, device_id={"blk": other}, device_id_type=pl.DeviceIdType.MESH
        )

    own = pltpu.make_async_copy(
        frames_ref.at[:, pl.ds(pl.multiple_of(me * span, span), span)], gathered.at[me], own_sem.at[0]
    )
    own.start()

    row_id = lax.broadcasted_iota(jnp.int32, (rows, rows), 0)
    col_id = lax.broadcasted_iota(jnp.int32, (rows, rows), 1)
    fetch_density.wait()
    density_row = density_vmem[...].astype(jnp.float32)
    density_col = jnp.sum(
        jnp.where(row_id == col_id, jnp.broadcast_to(density_row, (rows, rows)), 0.0),
        axis=1,
        keepdims=True,
    )
    fetch_basis.wait()
    own_basis = basis_vmem[...].astype(jnp.float32)
    own_wide = jnp.concatenate(
        [own_basis, jnp.broadcast_to(density_col, (rows, LANES - width))], axis=1
    )
    aux[me] = own_wide.astype(jnp.bfloat16)

    pl.semaphore_wait(barrier, n - 1)

    def send(src, dst, slot, other):
        pltpu.make_async_remote_copy(
            src_ref=src,
            dst_ref=dst,
            send_sem=send_sem.at[slot],
            recv_sem=recv_sem.at[slot],
            device_id={"blk": other},
            device_id_type=pl.DeviceIdType.MESH,
        ).start()

    def wait_all(buffer, sem):
        part = buffer.at[pl.ds(0, n - 1)]
        pltpu.make_async_copy(part, part, sem).wait()

    for other in others:
        send(
            frames_ref.at[:, pl.ds(pl.multiple_of(other * span, span), span)],
            gathered.at[me],
            0,
            other,
        )
    for other in others:
        send(aux.at[me], aux.at[me], 1, other)

    wait_all(aux, recv_sem.at[1])
    wide = aux[...].astype(jnp.float32).reshape(total, LANES)
    eye = lax.broadcasted_iota(jnp.int32, (total, total), 0) == lax.broadcasted_iota(
        jnp.int32, (total, total), 1
    )
    density_all = jnp.sum(jnp.where(eye, wide[:, width : width + 1], 0.0), axis=0, keepdims=True)
    vectors = wide[:, :width]
    twice = jnp.concatenate([vectors, vectors], axis=1).astype(jnp.bfloat16)
    overlap = lax.dot_general(
        own_basis.astype(jnp.bfloat16),
        vectors.astype(jnp.bfloat16),
        (((1,), (1,)), ((), ())),
        preferred_element_type=jnp.float32,
    )
    overlap_high = overlap.astype(jnp.bfloat16).astype(jnp.float32)
    onto = jnp.concatenate(
        [jnp.transpose(wide)[:width], overlap_high, overlap - overlap_high], axis=0
    ).astype(jnp.bfloat16)

    own.wait()
    wait_all(gathered, recv_sem.at[0])
    block = gathered[...].reshape(total, span)
    gram = lax.dot_general(
        block, block, (((1,), (1,)), ((), ())), preferred_element_type=jnp.float32
    )
    diagonal = jnp.where(eye, gram, 0.0)
    dist = (
        jnp.sum(diagonal, axis=1, keepdims=True)
        + jnp.sum(diagonal, axis=0, keepdims=True)
        - 2.0 * gram
    )
    partial[...] = dist.reshape(n, rows, total)
    for other in others:
        send(partial.at[other], arrived.at[me], 2, other)
    arrived[me] = partial[me]
    wait_all(arrived, recv_sem.at[2])

    squared_dist = jnp.sum(arrived[...], axis=0)
    weight = (jnp.exp(-squared_dist / features) * density_all).astype(jnp.bfloat16)
    numer = jnp.dot(weight, twice, preferred_element_type=jnp.float32)
    totals = jnp.sum(weight.astype(jnp.float32), axis=1, keepdims=True)
    own_applied = numer / totals
    high = own_applied.astype(jnp.bfloat16).astype(jnp.float32)
    lane = lax.broadcasted_iota(jnp.int32, (rows, LANES), 1)
    applied[me] = jnp.where(lane < width, high, own_applied - high).astype(jnp.bfloat16)
    for other in others:
        send(applied.at[me], applied.at[me], 3, other)
    wait_all(applied, recv_sem.at[3])

    products = jnp.dot(
        onto, applied[...].reshape(total, LANES), preferred_element_type=jnp.float32
    )
    products = products[:, :width] + products[:, width : 2 * width]
    both_ref[:width] = products[:width]
    projection = products[width : width + rows] + products[width + rows :]
    both_ref[width:] = own_applied[:, :width] - projection / total

    wait_all(gathered, send_sem.at[0])
    wait_all(aux, send_sem.at[1])
    wait_all(arrived, send_sem.at[2])
    wait_all(applied, send_sem.at[3])


def finish(width, both_ref, residual_ref, coef_ref):
    coef_ref[...] = both_ref[:width]
    residual_ref[...] = both_ref[width:].astype(jnp.bfloat16)


def shards(n, frames, basis, density):
    rows, features = frames.shape
    width = basis.shape[1]
    total = n * rows
    vmem = pl.BlockSpec(memory_space=pltpu.VMEM)
    operands = (frames, basis, density.reshape(1, rows))
    both = pl.pallas_call(
        functools.partial(kernel, n),
        out_shape=jax.ShapeDtypeStruct((width + rows, width), jnp.float32),
        in_specs=[pl.BlockSpec(memory_space=pltpu.HBM)] * 3,
        out_specs=vmem,
        scratch_shapes=[
            pltpu.VMEM((n, rows, features // n), jnp.bfloat16),
            pltpu.VMEM((n, rows, LANES), jnp.bfloat16),
            pltpu.VMEM((n, rows, total), jnp.float32),
            pltpu.VMEM((n, rows, total), jnp.float32),
            pltpu.VMEM((n, rows, LANES), jnp.bfloat16),
            pltpu.VMEM((rows, width), jnp.bfloat16),
            pltpu.VMEM((1, rows), jnp.bfloat16),
            pltpu.SemaphoreType.DMA((3,)),
            pltpu.SemaphoreType.DMA((4,)),
            pltpu.SemaphoreType.DMA((4,)),
        ],
        compiler_params=pltpu.CompilerParams(
            collective_id=0, has_side_effects=True, vmem_limit_bytes=32 * 1024 * 1024
        ),
        cost_estimate=pl.CostEstimate(
            flops=2 * total * total * (features // n),
            bytes_accessed=2 * rows * features,
            transcendentals=rows * total,
        ),
    )(*(pltpu.with_memory_space_constraint(x, pltpu.HBM) for x in operands))
    return pl.pallas_call(
        functools.partial(finish, width),
        out_shape=(
            jax.ShapeDtypeStruct((rows, width), jnp.bfloat16),
            jax.ShapeDtypeStruct((width, width), jnp.float32),
        ),
        in_specs=[vmem],
        out_specs=(vmem, vmem),
    )(both)


def solution(mesh):
    placed = (P(("groups", "blk"), None), P(("groups", "blk"), None), P(("groups", "blk")))
    return jax.shard_map(
        functools.partial(shards, mesh.shape["blk"]),
        mesh=mesh,
        in_specs=placed,
        out_specs=(P(("groups", "blk"), None), P("groups", None)),
        check_vma=False,
    )
```

```python
import functools

import jax
import jax.numpy as jnp
from jax import lax
from jax.experimental import pallas as pl
from jax.experimental.pallas import tpu as pltpu
from jax.sharding import PartitionSpec as P

LANES = 128


def partners(me, n):
    half = n // 2
    upper = me >= half
    place = jnp.where(upper, me - half, me)
    mine = jnp.where(upper, half, 0)
    turned = [place] + [
        jnp.where(place >= half - j, place + j - half, place + j) for j in range(1, half)
    ]
    return [half - mine + t for t in turned] + [mine + t for t in turned[1:]]


def kernel(
    n,
    frames_ref,
    basis_ref,
    density_ref,
    residual_ref,
    coef_ref,
    gathered,
    aux,
    partial,
    arrived,
    applied,
    basis_vmem,
    density_vmem,
    own_sem,
    send_sem,
    recv_sem,
):
    me = lax.axis_index("blk")
    rows, features = frames_ref.shape
    width = basis_ref.shape[1]
    span = features // n
    total = n * rows
    others = partners(me, n)

    fetch_basis = pltpu.make_async_copy(basis_ref, basis_vmem, own_sem.at[1])
    fetch_basis.start()
    fetch_density = pltpu.make_async_copy(density_ref, density_vmem, own_sem.at[2])
    fetch_density.start()

    barrier = pltpu.get_barrier_semaphore()
    for other in others:
        pl.semaphore_signal(
            barrier, inc=1, device_id={"blk": other}, device_id_type=pl.DeviceIdType.MESH
        )

    own = pltpu.make_async_copy(
        frames_ref.at[:, pl.ds(pl.multiple_of(me * span, span), span)], gathered.at[me], own_sem.at[0]
    )
    own.start()

    row_id = lax.broadcasted_iota(jnp.int32, (rows, rows), 0)
    col_id = lax.broadcasted_iota(jnp.int32, (rows, rows), 1)
    fetch_density.wait()
    density_row = density_vmem[...].astype(jnp.float32)
    density_col = jnp.sum(
        jnp.where(row_id == col_id, jnp.broadcast_to(density_row, (rows, rows)), 0.0),
        axis=1,
        keepdims=True,
    )
    fetch_basis.wait()
    own_basis = basis_vmem[...].astype(jnp.float32)
    own_wide = jnp.concatenate(
        [own_basis, jnp.broadcast_to(density_col, (rows, LANES - width))], axis=1
    )
    aux[me] = own_wide.astype(jnp.bfloat16)

    pl.semaphore_wait(barrier, n - 1)

    def send(src, dst, slot, other):
        pltpu.make_async_remote_copy(
            src_ref=src,
            dst_ref=dst,
            send_sem=send_sem.at[slot],
            recv_sem=recv_sem.at[slot],
            device_id={"blk": other},
            device_id_type=pl.DeviceIdType.MESH,
        ).start()

    def wait_all(buffer, sem):
        part = buffer.at[pl.ds(0, n - 1)]
        pltpu.make_async_copy(part, part, sem).wait()

    for other in others:
        send(
            frames_ref.at[:, pl.ds(pl.multiple_of(other * span, span), span)],
            gathered.at[me],
            0,
            other,
        )
    for other in others:
        send(aux.at[me], aux.at[me], 1, other)

    wait_all(aux, recv_sem.at[1])
    wide = aux[...].astype(jnp.float32).reshape(total, LANES)
    eye = lax.broadcasted_iota(jnp.int32, (total, total), 0) == lax.broadcasted_iota(
        jnp.int32, (total, total), 1
    )
    density_all = jnp.sum(jnp.where(eye, wide[:, width : width + 1], 0.0), axis=0, keepdims=True)
    vectors = wide[:, :width]
    twice = jnp.concatenate([vectors, vectors], axis=1).astype(jnp.bfloat16)
    overlap = lax.dot_general(
        own_basis.astype(jnp.bfloat16),
        vectors.astype(jnp.bfloat16),
        (((1,), (1,)), ((), ())),
        preferred_element_type=jnp.float32,
    )
    overlap_high = overlap.astype(jnp.bfloat16).astype(jnp.float32)
    onto = jnp.concatenate(
        [jnp.transpose(wide)[:width], overlap_high, overlap - overlap_high], axis=0
    ).astype(jnp.bfloat16)

    own.wait()
    wait_all(gathered, recv_sem.at[0])
    block = gathered[...].reshape(total, span)
    gram = lax.dot_general(
        block, block, (((1,), (1,)), ((), ())), preferred_element_type=jnp.float32
    )
    diagonal = jnp.where(eye, gram, 0.0)
    dist = (
        jnp.sum(diagonal, axis=1, keepdims=True)
        + jnp.sum(diagonal, axis=0, keepdims=True)
        - 2.0 * gram
    )
    partial[...] = dist.reshape(n, rows, total).astype(jnp.bfloat16)
    for other in others:
        send(partial.at[other], arrived.at[me], 2, other)
    arrived[me] = partial[me]
    wait_all(arrived, recv_sem.at[2])

    squared_dist = jnp.sum(arrived[...].astype(jnp.float32), axis=0)
    weight = (jnp.exp(-squared_dist / features) * density_all).astype(jnp.bfloat16)
    numer = jnp.dot(weight, twice, preferred_element_type=jnp.float32)
    totals = jnp.sum(weight.astype(jnp.float32), axis=1, keepdims=True)
    own_applied = numer / totals
    high = own_applied.astype(jnp.bfloat16).astype(jnp.float32)
    lane = lax.broadcasted_iota(jnp.int32, (rows, LANES), 1)
    applied[me] = jnp.where(lane < width, high, own_applied - high).astype(jnp.bfloat16)
    for other in others:
        send(applied.at[me], applied.at[me], 3, other)
    wait_all(applied, recv_sem.at[3])

    products = jnp.dot(
        onto, applied[...].reshape(total, LANES), preferred_element_type=jnp.float32
    )
    products = products[:, :width] + products[:, width : 2 * width]
    coef_ref[...] = products[:width]
    projection = products[width : width + rows] + products[width + rows :]
    residual_ref[...] = (own_applied[:, :width] - projection / total).astype(jnp.bfloat16)

    wait_all(gathered, send_sem.at[0])
    wait_all(aux, send_sem.at[1])
    wait_all(arrived, send_sem.at[2])
    wait_all(applied, send_sem.at[3])


def shards(n, frames, basis, density):
    rows, features = frames.shape
    width = basis.shape[1]
    total = n * rows
    vmem = pl.BlockSpec(memory_space=pltpu.VMEM)
    operands = (frames, basis, density.reshape(1, rows))
    return pl.pallas_call(
        functools.partial(kernel, n),
        out_shape=(
            jax.ShapeDtypeStruct((rows, width), jnp.bfloat16),
            jax.ShapeDtypeStruct((width, width), jnp.float32),
        ),
        in_specs=[pl.BlockSpec(memory_space=pltpu.HBM)] * 3,
        out_specs=(vmem, vmem),
        scratch_shapes=[
            pltpu.VMEM((n, rows, features // n), jnp.bfloat16),
            pltpu.VMEM((n, rows, LANES), jnp.bfloat16),
            pltpu.VMEM((n, rows, total), jnp.bfloat16),
            pltpu.VMEM((n, rows, total), jnp.bfloat16),
            pltpu.VMEM((n, rows, LANES), jnp.bfloat16),
            pltpu.VMEM((rows, width), jnp.bfloat16),
            pltpu.VMEM((1, rows), jnp.bfloat16),
            pltpu.SemaphoreType.DMA((3,)),
            pltpu.SemaphoreType.DMA((4,)),
            pltpu.SemaphoreType.DMA((4,)),
        ],
        compiler_params=pltpu.CompilerParams(
            collective_id=0, has_side_effects=True, vmem_limit_bytes=32 * 1024 * 1024
        ),
        cost_estimate=pl.CostEstimate(
            flops=2 * total * total * (features // n),
            bytes_accessed=2 * rows * features,
            transcendentals=rows * total,
        ),
    )(*(pltpu.with_memory_space_constraint(x, pltpu.HBM) for x in operands))


def solution(mesh):
    placed = (P(("groups", "blk"), None), P(("groups", "blk"), None), P(("groups", "blk")))
    return jax.shard_map(
        functools.partial(shards, mesh.shape["blk"]),
        mesh=mesh,
        in_specs=placed,
        out_specs=(P(("groups", "blk"), None), P("groups", None)),
        check_vma=False,
    )
```

```python
import functools

import jax
import jax.numpy as jnp
from jax import lax
from jax.experimental import pallas as pl
from jax.experimental.pallas import tpu as pltpu
from jax.sharding import PartitionSpec as P

LANES = 128


def partners(me, n):
    half = n // 2
    upper = me >= half
    place = jnp.where(upper, me - half, me)
    mine = jnp.where(upper, half, 0)
    turned = [place] + [
        jnp.where(place >= half - j, place + j - half, place + j) for j in range(1, half)
    ]
    return [half - mine + t for t in turned] + [mine + t for t in turned[1:]]


def kernel(
    n,
    frames_ref,
    basis_ref,
    density_ref,
    residual_ref,
    coef_ref,
    gathered,
    aux,
    partial,
    arrived,
    applied,
    basis_vmem,
    density_vmem,
    staged,
    own_sem,
    send_sem,
    recv_sem,
):
    me = lax.axis_index("blk")
    rows, features = frames_ref.shape
    width = basis_ref.shape[1]
    span = features // n
    total = n * rows
    others = partners(me, n)

    stage = pltpu.make_async_copy(frames_ref, staged, own_sem.at[0])
    stage.start()
    fetch_basis = pltpu.make_async_copy(basis_ref, basis_vmem, own_sem.at[1])
    fetch_basis.start()
    fetch_density = pltpu.make_async_copy(density_ref, density_vmem, own_sem.at[2])
    fetch_density.start()

    barrier = pltpu.get_barrier_semaphore()
    for other in others:
        pl.semaphore_signal(
            barrier, inc=1, device_id={"blk": other}, device_id_type=pl.DeviceIdType.MESH
        )

    pl.semaphore_wait(barrier, n - 1)

    def send(src, dst, slot, other):
        pltpu.make_async_remote_copy(
            src_ref=src,
            dst_ref=dst,
            send_sem=send_sem.at[slot],
            recv_sem=recv_sem.at[slot],
            device_id={"blk": other},
            device_id_type=pl.DeviceIdType.MESH,
        ).start()

    def wait_all(buffer, sem):
        part = buffer.at[pl.ds(0, n - 1)]
        pltpu.make_async_copy(part, part, sem).wait()

    stage.wait()
    for other in others:
        send(
            staged.at[:, pl.ds(pl.multiple_of(other * span, span), span)],
            gathered.at[me],
            0,
            other,
        )
    own = pltpu.make_async_copy(
        staged.at[:, pl.ds(pl.multiple_of(me * span, span), span)], gathered.at[me], own_sem.at[3]
    )
    own.start()

    row_id = lax.broadcasted_iota(jnp.int32, (rows, rows), 0)
    col_id = lax.broadcasted_iota(jnp.int32, (rows, rows), 1)
    fetch_density.wait()
    density_row = density_vmem[...].astype(jnp.float32)
    density_col = jnp.sum(
        jnp.where(row_id == col_id, jnp.broadcast_to(density_row, (rows, rows)), 0.0),
        axis=1,
        keepdims=True,
    )
    fetch_basis.wait()
    own_basis = basis_vmem[...].astype(jnp.float32)
    own_wide = jnp.concatenate(
        [own_basis, jnp.broadcast_to(density_col, (rows, LANES - width))], axis=1
    )
    aux[me] = own_wide.astype(jnp.bfloat16)
    for other in others:
        send(aux.at[me], aux.at[me], 1, other)

    eye = lax.broadcasted_iota(jnp.int32, (total, total), 0) == lax.broadcasted_iota(
        jnp.int32, (total, total), 1
    )
    own.wait()
    wait_all(gathered, recv_sem.at[0])
    block = gathered[...].reshape(total, span)
    gram = lax.dot_general(
        block, block, (((1,), (1,)), ((), ())), preferred_element_type=jnp.float32
    )
    diagonal = jnp.where(eye, gram, 0.0)
    dist = (
        jnp.sum(diagonal, axis=1, keepdims=True)
        + jnp.sum(diagonal, axis=0, keepdims=True)
        - 2.0 * gram
    )
    partial[...] = dist.reshape(n, rows, total).astype(jnp.bfloat16)
    for other in others:
        send(partial.at[other], arrived.at[me], 2, other)
    arrived[me] = partial[me]

    wait_all(aux, recv_sem.at[1])
    wide = aux[...].astype(jnp.float32).reshape(total, LANES)
    density_all = jnp.sum(jnp.where(eye, wide[:, width : width + 1], 0.0), axis=0, keepdims=True)
    vectors = wide[:, :width]
    twice = jnp.concatenate([vectors, vectors], axis=1).astype(jnp.bfloat16)

    wait_all(arrived, recv_sem.at[2])

    squared_dist = jnp.sum(arrived[...].astype(jnp.float32), axis=0)
    weight = (jnp.exp(-squared_dist / features) * density_all).astype(jnp.bfloat16)
    numer = jnp.dot(weight, twice, preferred_element_type=jnp.float32)
    totals = jnp.sum(weight.astype(jnp.float32), axis=1, keepdims=True)
    own_applied = numer / totals
    high = own_applied.astype(jnp.bfloat16).astype(jnp.float32)
    lane = lax.broadcasted_iota(jnp.int32, (rows, LANES), 1)
    applied[me] = jnp.where(lane < width, high, own_applied - high).astype(jnp.bfloat16)
    for other in others:
        send(applied.at[me], applied.at[me], 3, other)

    overlap = lax.dot_general(
        own_basis.astype(jnp.bfloat16),
        vectors.astype(jnp.bfloat16),
        (((1,), (1,)), ((), ())),
        preferred_element_type=jnp.float32,
    )
    overlap_high = overlap.astype(jnp.bfloat16).astype(jnp.float32)
    onto = jnp.concatenate(
        [jnp.transpose(wide)[:width], overlap_high, overlap - overlap_high], axis=0
    ).astype(jnp.bfloat16)

    wait_all(applied, recv_sem.at[3])

    products = jnp.dot(
        onto, applied[...].reshape(total, LANES), preferred_element_type=jnp.float32
    )
    products = products[:, :width] + products[:, width : 2 * width]
    coef_ref[...] = products[:width]
    projection = products[width : width + rows] + products[width + rows :]
    residual_ref[...] = (own_applied[:, :width] - projection / total).astype(jnp.bfloat16)

    wait_all(gathered, send_sem.at[0])
    wait_all(aux, send_sem.at[1])
    wait_all(arrived, send_sem.at[2])
    wait_all(applied, send_sem.at[3])


def shards(n, frames, basis, density):
    rows, features = frames.shape
    width = basis.shape[1]
    total = n * rows
    vmem = pl.BlockSpec(memory_space=pltpu.VMEM)
    operands = (frames, basis, density.reshape(1, rows))
    return pl.pallas_call(
        functools.partial(kernel, n),
        out_shape=(
            jax.ShapeDtypeStruct((rows, width), jnp.bfloat16),
            jax.ShapeDtypeStruct((width, width), jnp.float32),
        ),
        in_specs=[pl.BlockSpec(memory_space=pltpu.HBM)] * 3,
        out_specs=(vmem, vmem),
        scratch_shapes=[
            pltpu.VMEM((n, rows, features // n), jnp.bfloat16),
            pltpu.VMEM((n, rows, LANES), jnp.bfloat16),
            pltpu.VMEM((n, rows, total), jnp.bfloat16),
            pltpu.VMEM((n, rows, total), jnp.bfloat16),
            pltpu.VMEM((n, rows, LANES), jnp.bfloat16),
            pltpu.VMEM((rows, width), jnp.bfloat16),
            pltpu.VMEM((1, rows), jnp.bfloat16),
            pltpu.VMEM((rows, features), jnp.bfloat16),
            pltpu.SemaphoreType.DMA((4,)),
            pltpu.SemaphoreType.DMA((4,)),
            pltpu.SemaphoreType.DMA((4,)),
        ],
        compiler_params=pltpu.CompilerParams(
            collective_id=0, has_side_effects=True, vmem_limit_bytes=32 * 1024 * 1024
        ),
        cost_estimate=pl.CostEstimate(
            flops=2 * total * total * (features // n),
            bytes_accessed=2 * rows * features,
            transcendentals=rows * total,
        ),
    )(*(pltpu.with_memory_space_constraint(x, pltpu.HBM) for x in operands))


def solution(mesh):
    placed = (P(("groups", "blk"), None), P(("groups", "blk"), None), P(("groups", "blk")))
    return jax.shard_map(
        functools.partial(shards, mesh.shape["blk"]),
        mesh=mesh,
        in_specs=placed,
        out_specs=(P(("groups", "blk"), None), P("groups", None)),
        check_vma=False,
    )
```

```python
import functools

import jax
import jax.numpy as jnp
from jax import lax
from jax.experimental import pallas as pl
from jax.experimental.pallas import tpu as pltpu
from jax.sharding import PartitionSpec as P

LANES = 128
CHUNKS = 2


def partners(me, n):
    half = n // 2
    upper = me >= half
    place = jnp.where(upper, me - half, me)
    mine = jnp.where(upper, half, 0)
    turned = [place] + [
        jnp.where(place >= half - j, place + j - half, place + j) for j in range(1, half)
    ]
    return [half - mine + t for t in turned] + [mine + t for t in turned[1:]]


def kernel(
    n,
    frames_ref,
    basis_ref,
    density_ref,
    residual_ref,
    coef_ref,
    gathered,
    aux,
    partial,
    arrived,
    applied,
    basis_vmem,
    density_vmem,
    staged,
    own_sem,
    send_sem,
    recv_sem,
):
    me = lax.axis_index("blk")
    rows, features = frames_ref.shape
    width = basis_ref.shape[1]
    span = features // n
    piece = span // CHUNKS
    total = n * rows
    others = partners(me, n)

    stage = pltpu.make_async_copy(frames_ref, staged, own_sem.at[0])
    stage.start()
    fetch_basis = pltpu.make_async_copy(basis_ref, basis_vmem, own_sem.at[1])
    fetch_basis.start()
    fetch_density = pltpu.make_async_copy(density_ref, density_vmem, own_sem.at[2])
    fetch_density.start()

    barrier = pltpu.get_barrier_semaphore()
    for other in others:
        pl.semaphore_signal(
            barrier, inc=1, device_id={"blk": other}, device_id_type=pl.DeviceIdType.MESH
        )

    pl.semaphore_wait(barrier, n - 1)

    def send(src, dst, slot, other):
        pltpu.make_async_remote_copy(
            src_ref=src,
            dst_ref=dst,
            send_sem=send_sem.at[slot],
            recv_sem=recv_sem.at[slot],
            device_id={"blk": other},
            device_id_type=pl.DeviceIdType.MESH,
        ).start()

    def wait_all(buffer, sem):
        part = buffer.at[pl.ds(0, n - 1)]
        pltpu.make_async_copy(part, part, sem).wait()

    stage.wait()
    def columns(owner, chunk):
        return staged.at[:, pl.ds(pl.multiple_of(owner * span + chunk * piece, piece), piece)]

    own = []
    for chunk in range(CHUNKS):
        for other in others:
            send(columns(other, chunk), gathered.at[chunk, me], 3 + chunk, other)
        own.append(
            pltpu.make_async_copy(
                columns(me, chunk), gathered.at[chunk, me], own_sem.at[3 + chunk]
            )
        )
        own[chunk].start()

    row_id = lax.broadcasted_iota(jnp.int32, (rows, rows), 0)
    col_id = lax.broadcasted_iota(jnp.int32, (rows, rows), 1)
    fetch_density.wait()
    density_row = density_vmem[...].astype(jnp.float32)
    density_col = jnp.sum(
        jnp.where(row_id == col_id, jnp.broadcast_to(density_row, (rows, rows)), 0.0),
        axis=1,
        keepdims=True,
    )
    fetch_basis.wait()
    own_basis = basis_vmem[...].astype(jnp.float32)
    own_wide = jnp.concatenate(
        [own_basis, jnp.broadcast_to(density_col, (rows, LANES - width))], axis=1
    )
    aux[me] = own_wide.astype(jnp.bfloat16)
    for other in others:
        send(aux.at[me], aux.at[me], 0, other)

    eye = lax.broadcasted_iota(jnp.int32, (total, total), 0) == lax.broadcasted_iota(
        jnp.int32, (total, total), 1
    )
    gram = jnp.zeros((total, total), jnp.float32)
    for chunk in range(CHUNKS):
        own[chunk].wait()
        wait_all(gathered.at[chunk], recv_sem.at[3 + chunk])
        block = gathered[chunk].reshape(total, piece)
        gram += lax.dot_general(
            block, block, (((1,), (1,)), ((), ())), preferred_element_type=jnp.float32
        )
    diagonal = jnp.where(eye, gram, 0.0)
    dist = (
        jnp.sum(diagonal, axis=1, keepdims=True)
        + jnp.sum(diagonal, axis=0, keepdims=True)
        - 2.0 * gram
    )
    partial[...] = dist.reshape(n, rows, total).astype(jnp.bfloat16)
    for other in others:
        send(partial.at[other], arrived.at[me], 1, other)
    arrived[me] = partial[me]

    wait_all(aux, recv_sem.at[0])
    wide = aux[...].astype(jnp.float32).reshape(total, LANES)
    density_all = jnp.sum(jnp.where(eye, wide[:, width : width + 1], 0.0), axis=0, keepdims=True)
    vectors = wide[:, :width]
    twice = jnp.concatenate([vectors, vectors], axis=1).astype(jnp.bfloat16)

    wait_all(arrived, recv_sem.at[1])

    squared_dist = jnp.sum(arrived[...].astype(jnp.float32), axis=0)
    weight = (jnp.exp(-squared_dist / features) * density_all).astype(jnp.bfloat16)
    numer = jnp.dot(weight, twice, preferred_element_type=jnp.float32)
    totals = jnp.sum(weight.astype(jnp.float32), axis=1, keepdims=True)
    own_applied = numer / totals
    high = own_applied.astype(jnp.bfloat16).astype(jnp.float32)
    lane = lax.broadcasted_iota(jnp.int32, (rows, LANES), 1)
    applied[me] = jnp.where(lane < width, high, own_applied - high).astype(jnp.bfloat16)
    for other in others:
        send(applied.at[me], applied.at[me], 2, other)

    overlap = lax.dot_general(
        own_basis.astype(jnp.bfloat16),
        vectors.astype(jnp.bfloat16),
        (((1,), (1,)), ((), ())),
        preferred_element_type=jnp.float32,
    )
    overlap_high = overlap.astype(jnp.bfloat16).astype(jnp.float32)
    onto = jnp.concatenate(
        [jnp.transpose(wide)[:width], overlap_high, overlap - overlap_high], axis=0
    ).astype(jnp.bfloat16)

    wait_all(applied, recv_sem.at[2])

    products = jnp.dot(
        onto, applied[...].reshape(total, LANES), preferred_element_type=jnp.float32
    )
    products = products[:, :width] + products[:, width : 2 * width]
    coef_ref[...] = products[:width]
    projection = products[width : width + rows] + products[width + rows :]
    residual_ref[...] = (own_applied[:, :width] - projection / total).astype(jnp.bfloat16)

    wait_all(aux, send_sem.at[0])
    wait_all(arrived, send_sem.at[1])
    wait_all(applied, send_sem.at[2])
    for chunk in range(CHUNKS):
        wait_all(gathered.at[chunk], send_sem.at[3 + chunk])


def shards(n, frames, basis, density):
    rows, features = frames.shape
    width = basis.shape[1]
    total = n * rows
    vmem = pl.BlockSpec(memory_space=pltpu.VMEM)
    operands = (frames, basis, density.reshape(1, rows))
    return pl.pallas_call(
        functools.partial(kernel, n),
        out_shape=(
            jax.ShapeDtypeStruct((rows, width), jnp.bfloat16),
            jax.ShapeDtypeStruct((width, width), jnp.float32),
        ),
        in_specs=[pl.BlockSpec(memory_space=pltpu.HBM)] * 3,
        out_specs=(vmem, vmem),
        scratch_shapes=[
            pltpu.VMEM((CHUNKS, n, rows, features // n // CHUNKS), jnp.bfloat16),
            pltpu.VMEM((n, rows, LANES), jnp.bfloat16),
            pltpu.VMEM((n, rows, total), jnp.bfloat16),
            pltpu.VMEM((n, rows, total), jnp.bfloat16),
            pltpu.VMEM((n, rows, LANES), jnp.bfloat16),
            pltpu.VMEM((rows, width), jnp.bfloat16),
            pltpu.VMEM((1, rows), jnp.bfloat16),
            pltpu.VMEM((rows, features), jnp.bfloat16),
            pltpu.SemaphoreType.DMA((3 + CHUNKS,)),
            pltpu.SemaphoreType.DMA((3 + CHUNKS,)),
            pltpu.SemaphoreType.DMA((3 + CHUNKS,)),
        ],
        compiler_params=pltpu.CompilerParams(
            collective_id=0, has_side_effects=True, vmem_limit_bytes=32 * 1024 * 1024
        ),
        cost_estimate=pl.CostEstimate(
            flops=2 * total * total * (features // n),
            bytes_accessed=2 * rows * features,
            transcendentals=rows * total,
        ),
    )(*(pltpu.with_memory_space_constraint(x, pltpu.HBM) for x in operands))


def solution(mesh):
    placed = (P(("groups", "blk"), None), P(("groups", "blk"), None), P(("groups", "blk")))
    return jax.shard_map(
        functools.partial(shards, mesh.shape["blk"]),
        mesh=mesh,
        in_specs=placed,
        out_specs=(P(("groups", "blk"), None), P("groups", None)),
        check_vma=False,
    )
```

```python
import functools

import jax
import jax.numpy as jnp
from jax import lax
from jax.experimental import pallas as pl
from jax.experimental.pallas import tpu as pltpu
from jax.sharding import PartitionSpec as P

LANES = 128


def for_partners(me, n, body):
    half = n // 2
    upper = me >= half
    place = jnp.where(upper, me - half, me)
    mine = jnp.where(upper, half, 0)

    @pl.loop(0, n - 1)
    def _(k):
        far = k < half
        turned = place + jnp.where(far, k, k - half + 1)
        turned = jnp.where(turned >= half, turned - half, turned)
        body(turned + jnp.where(far, half - mine, mine))


def kernel(
    n,
    frames_ref,
    basis_ref,
    density_ref,
    residual_ref,
    coef_ref,
    gathered,
    aux,
    partial,
    arrived,
    applied,
    basis_vmem,
    density_vmem,
    staged,
    own_sem,
    send_sem,
    recv_sem,
):
    me = lax.axis_index("blk")
    rows, features = frames_ref.shape
    width = basis_ref.shape[1]
    span = features // n
    total = n * rows

    stage = pltpu.make_async_copy(frames_ref, staged, own_sem.at[0])
    stage.start()
    fetch_basis = pltpu.make_async_copy(basis_ref, basis_vmem, own_sem.at[1])
    fetch_basis.start()
    fetch_density = pltpu.make_async_copy(density_ref, density_vmem, own_sem.at[2])
    fetch_density.start()

    barrier = pltpu.get_barrier_semaphore()
    def greet(other):
        pl.semaphore_signal(
            barrier, inc=1, device_id={"blk": other}, device_id_type=pl.DeviceIdType.MESH
        )

    for_partners(me, n, greet)
    pl.semaphore_wait(barrier, n - 1)

    def send(src, dst, slot, other):
        pltpu.make_async_remote_copy(
            src_ref=src,
            dst_ref=dst,
            send_sem=send_sem.at[slot],
            recv_sem=recv_sem.at[slot],
            device_id={"blk": other},
            device_id_type=pl.DeviceIdType.MESH,
        ).start()

    def wait_all(buffer, sem):
        part = buffer.at[pl.ds(0, n - 1)]
        pltpu.make_async_copy(part, part, sem).wait()

    stage.wait()

    def columns(owner):
        return staged.at[:, pl.ds(pl.multiple_of(owner * span, span), span)]

    for_partners(me, n, lambda other: send(columns(other), gathered.at[me], 0, other))
    own = pltpu.make_async_copy(columns(me), gathered.at[me], own_sem.at[3])
    own.start()

    row_id = lax.broadcasted_iota(jnp.int32, (rows, rows), 0)
    col_id = lax.broadcasted_iota(jnp.int32, (rows, rows), 1)
    fetch_density.wait()
    density_row = density_vmem[...].astype(jnp.float32)
    density_col = jnp.sum(
        jnp.where(row_id == col_id, jnp.broadcast_to(density_row, (rows, rows)), 0.0),
        axis=1,
        keepdims=True,
    )
    fetch_basis.wait()
    own_basis = basis_vmem[...].astype(jnp.float32)
    own_wide = jnp.concatenate(
        [own_basis, jnp.broadcast_to(density_col, (rows, LANES - width))], axis=1
    )
    aux[me] = own_wide.astype(jnp.bfloat16)
    for_partners(me, n, lambda other: send(aux.at[me], aux.at[me], 1, other))

    eye = lax.broadcasted_iota(jnp.int32, (total, total), 0) == lax.broadcasted_iota(
        jnp.int32, (total, total), 1
    )
    own.wait()
    wait_all(gathered, recv_sem.at[0])
    block = gathered[...].reshape(total, span)
    gram = lax.dot_general(
        block, block, (((1,), (1,)), ((), ())), preferred_element_type=jnp.float32
    )
    diagonal = jnp.where(eye, gram, 0.0)
    dist = (
        jnp.sum(diagonal, axis=1, keepdims=True)
        + jnp.sum(diagonal, axis=0, keepdims=True)
        - 2.0 * gram
    )
    partial[...] = dist.reshape(n, rows, total).astype(jnp.bfloat16)
    for_partners(me, n, lambda other: send(partial.at[other], arrived.at[me], 2, other))
    arrived[me] = partial[me]

    wait_all(aux, recv_sem.at[1])
    wide = aux[...].astype(jnp.float32).reshape(total, LANES)
    density_all = jnp.sum(jnp.where(eye, wide[:, width : width + 1], 0.0), axis=0, keepdims=True)
    vectors = wide[:, :width]
    twice = jnp.concatenate([vectors, vectors], axis=1).astype(jnp.bfloat16)

    wait_all(arrived, recv_sem.at[2])

    squared_dist = jnp.sum(arrived[...].astype(jnp.float32), axis=0)
    weight = (jnp.exp(-squared_dist / features) * density_all).astype(jnp.bfloat16)
    numer = jnp.dot(weight, twice, preferred_element_type=jnp.float32)
    totals = jnp.sum(weight.astype(jnp.float32), axis=1, keepdims=True)
    own_applied = numer / totals
    high = own_applied.astype(jnp.bfloat16).astype(jnp.float32)
    lane = lax.broadcasted_iota(jnp.int32, (rows, LANES), 1)
    applied[me] = jnp.where(lane < width, high, own_applied - high).astype(jnp.bfloat16)
    for_partners(me, n, lambda other: send(applied.at[me], applied.at[me], 3, other))

    overlap = lax.dot_general(
        own_basis.astype(jnp.bfloat16),
        vectors.astype(jnp.bfloat16),
        (((1,), (1,)), ((), ())),
        preferred_element_type=jnp.float32,
    )
    overlap_high = overlap.astype(jnp.bfloat16).astype(jnp.float32)
    onto = jnp.concatenate(
        [jnp.transpose(wide)[:width], overlap_high, overlap - overlap_high], axis=0
    ).astype(jnp.bfloat16)

    wait_all(applied, recv_sem.at[3])

    products = jnp.dot(
        onto, applied[...].reshape(total, LANES), preferred_element_type=jnp.float32
    )
    products = products[:, :width] + products[:, width : 2 * width]
    coef_ref[...] = products[:width]
    projection = products[width : width + rows] + products[width + rows :]
    residual_ref[...] = (own_applied[:, :width] - projection / total).astype(jnp.bfloat16)

    wait_all(gathered, send_sem.at[0])
    wait_all(aux, send_sem.at[1])
    wait_all(arrived, send_sem.at[2])
    wait_all(applied, send_sem.at[3])


def shards(n, frames, basis, density):
    rows, features = frames.shape
    width = basis.shape[1]
    total = n * rows
    vmem = pl.BlockSpec(memory_space=pltpu.VMEM)
    operands = (frames, basis, density.reshape(1, rows))
    return pl.pallas_call(
        functools.partial(kernel, n),
        out_shape=(
            jax.ShapeDtypeStruct((rows, width), jnp.bfloat16),
            jax.ShapeDtypeStruct((width, width), jnp.float32),
        ),
        in_specs=[pl.BlockSpec(memory_space=pltpu.HBM)] * 3,
        out_specs=(vmem, vmem),
        scratch_shapes=[
            pltpu.VMEM((n, rows, features // n), jnp.bfloat16),
            pltpu.VMEM((n, rows, LANES), jnp.bfloat16),
            pltpu.VMEM((n, rows, total), jnp.bfloat16),
            pltpu.VMEM((n, rows, total), jnp.bfloat16),
            pltpu.VMEM((n, rows, LANES), jnp.bfloat16),
            pltpu.VMEM((rows, width), jnp.bfloat16),
            pltpu.VMEM((1, rows), jnp.bfloat16),
            pltpu.VMEM((rows, features), jnp.bfloat16),
            pltpu.SemaphoreType.DMA((4,)),
            pltpu.SemaphoreType.DMA((4,)),
            pltpu.SemaphoreType.DMA((4,)),
        ],
        compiler_params=pltpu.CompilerParams(
            collective_id=0, has_side_effects=True, vmem_limit_bytes=32 * 1024 * 1024
        ),
        cost_estimate=pl.CostEstimate(
            flops=2 * total * total * (features // n),
            bytes_accessed=2 * rows * features,
            transcendentals=rows * total,
        ),
    )(*(pltpu.with_memory_space_constraint(x, pltpu.HBM) for x in operands))


def solution(mesh):
    placed = (P(("groups", "blk"), None), P(("groups", "blk"), None), P(("groups", "blk")))
    return jax.shard_map(
        functools.partial(shards, mesh.shape["blk"]),
        mesh=mesh,
        in_specs=placed,
        out_specs=(P(("groups", "blk"), None), P("groups", None)),
        check_vma=False,
    )
```

```python
import functools

import jax
import jax.numpy as jnp
from jax import lax
from jax.experimental import pallas as pl
from jax.experimental.pallas import tpu as pltpu
from jax.sharding import PartitionSpec as P

LANES = 128


def partners(me, n):
    half = n // 2
    upper = me >= half
    place = jnp.where(upper, me - half, me)
    mine = jnp.where(upper, half, 0)
    turned = [place] + [
        jnp.where(place >= half - j, place + j - half, place + j) for j in range(1, half)
    ]
    return [half - mine + t for t in turned] + [mine + t for t in turned[1:]]


def alternate(others):
    half = (len(others) + 1) // 2
    far, near = others[:half], others[half:]
    return [pick for pair in zip(far, near) for pick in pair] + [far[-1]]


def kernel(
    n,
    frames_ref,
    basis_ref,
    density_ref,
    residual_ref,
    coef_ref,
    gathered,
    aux,
    partial,
    arrived,
    applied,
    basis_vmem,
    density_vmem,
    staged,
    own_sem,
    send_sem,
    recv_sem,
):
    me = lax.axis_index("blk")
    rows, features = frames_ref.shape
    width = basis_ref.shape[1]
    span = features // n
    total = n * rows
    others = partners(me, n)

    barrier = pltpu.get_barrier_semaphore()
    for other in others:
        pl.semaphore_signal(
            barrier, inc=1, device_id={"blk": other}, device_id_type=pl.DeviceIdType.MESH
        )

    stage = pltpu.make_async_copy(frames_ref, staged, own_sem.at[0])
    stage.start()
    fetch_basis = pltpu.make_async_copy(basis_ref, basis_vmem, own_sem.at[1])
    fetch_basis.start()
    fetch_density = pltpu.make_async_copy(density_ref, density_vmem, own_sem.at[2])
    fetch_density.start()

    pl.semaphore_wait(barrier, n - 1)

    def send(src, dst, slot, other):
        pltpu.make_async_remote_copy(
            src_ref=src,
            dst_ref=dst,
            send_sem=send_sem.at[slot],
            recv_sem=recv_sem.at[slot],
            device_id={"blk": other},
            device_id_type=pl.DeviceIdType.MESH,
        ).start()

    def wait_all(buffer, sem):
        part = buffer.at[pl.ds(0, n - 1)]
        pltpu.make_async_copy(part, part, sem).wait()

    stage.wait()
    for other in alternate(others):
        send(
            staged.at[:, pl.ds(pl.multiple_of(other * span, span), span)],
            gathered.at[me],
            0,
            other,
        )
    own = pltpu.make_async_copy(
        staged.at[:, pl.ds(pl.multiple_of(me * span, span), span)], gathered.at[me], own_sem.at[3]
    )
    own.start()

    row_id = lax.broadcasted_iota(jnp.int32, (rows, rows), 0)
    col_id = lax.broadcasted_iota(jnp.int32, (rows, rows), 1)
    fetch_density.wait()
    density_row = density_vmem[...].astype(jnp.float32)
    density_col = jnp.sum(
        jnp.where(row_id == col_id, jnp.broadcast_to(density_row, (rows, rows)), 0.0),
        axis=1,
        keepdims=True,
    )
    fetch_basis.wait()
    own_basis = basis_vmem[...].astype(jnp.float32)
    own_wide = jnp.concatenate(
        [own_basis, jnp.broadcast_to(density_col, (rows, LANES - width))], axis=1
    )
    aux[me] = own_wide.astype(jnp.bfloat16)
    for other in others:
        send(aux.at[me], aux.at[me], 1, other)

    eye = lax.broadcasted_iota(jnp.int32, (total, total), 0) == lax.broadcasted_iota(
        jnp.int32, (total, total), 1
    )
    own.wait()
    wait_all(gathered, recv_sem.at[0])
    block = gathered[...].reshape(total, span)
    gram = lax.dot_general(
        block, block, (((1,), (1,)), ((), ())), preferred_element_type=jnp.float32
    )
    diagonal = jnp.where(eye, gram, 0.0)
    dist = (
        jnp.sum(diagonal, axis=1, keepdims=True)
        + jnp.sum(diagonal, axis=0, keepdims=True)
        - 2.0 * gram
    )
    partial[...] = dist.reshape(n, rows, total).astype(jnp.bfloat16)
    for other in others:
        send(partial.at[other], arrived.at[me], 2, other)
    arrived[me] = partial[me]

    wait_all(aux, recv_sem.at[1])
    wide = aux[...].astype(jnp.float32).reshape(total, LANES)
    density_all = jnp.sum(jnp.where(eye, wide[:, width : width + 1], 0.0), axis=0, keepdims=True)
    vectors = wide[:, :width]
    twice = jnp.concatenate([vectors, vectors], axis=1).astype(jnp.bfloat16)

    wait_all(arrived, recv_sem.at[2])

    squared_dist = jnp.sum(arrived[...].astype(jnp.float32), axis=0)
    weight = (jnp.exp(-squared_dist / features) * density_all).astype(jnp.bfloat16)
    numer = jnp.dot(weight, twice, preferred_element_type=jnp.float32)
    totals = jnp.sum(weight.astype(jnp.float32), axis=1, keepdims=True)
    own_applied = numer / totals
    high = own_applied.astype(jnp.bfloat16).astype(jnp.float32)
    lane = lax.broadcasted_iota(jnp.int32, (rows, LANES), 1)
    applied[me] = jnp.where(lane < width, high, own_applied - high).astype(jnp.bfloat16)
    for other in others:
        send(applied.at[me], applied.at[me], 3, other)

    overlap = lax.dot_general(
        own_basis.astype(jnp.bfloat16),
        vectors.astype(jnp.bfloat16),
        (((1,), (1,)), ((), ())),
        preferred_element_type=jnp.float32,
    )
    overlap_high = overlap.astype(jnp.bfloat16).astype(jnp.float32)
    onto = jnp.concatenate(
        [jnp.transpose(wide)[:width], overlap_high, overlap - overlap_high], axis=0
    ).astype(jnp.bfloat16)

    wait_all(applied, recv_sem.at[3])

    products = jnp.dot(
        onto, applied[...].reshape(total, LANES), preferred_element_type=jnp.float32
    )
    products = products[:, :width] + products[:, width : 2 * width]
    coef_ref[...] = products[:width]
    projection = products[width : width + rows] + products[width + rows :]
    residual_ref[...] = (own_applied[:, :width] - projection / total).astype(jnp.bfloat16)

    wait_all(gathered, send_sem.at[0])
    wait_all(aux, send_sem.at[1])
    wait_all(arrived, send_sem.at[2])
    wait_all(applied, send_sem.at[3])


def shards(n, frames, basis, density):
    rows, features = frames.shape
    width = basis.shape[1]
    total = n * rows
    vmem = pl.BlockSpec(memory_space=pltpu.VMEM)
    operands = (frames, basis, density.reshape(1, rows))
    return pl.pallas_call(
        functools.partial(kernel, n),
        out_shape=(
            jax.ShapeDtypeStruct((rows, width), jnp.bfloat16),
            jax.ShapeDtypeStruct((width, width), jnp.float32),
        ),
        in_specs=[pl.BlockSpec(memory_space=pltpu.HBM)] * 3,
        out_specs=(vmem, vmem),
        scratch_shapes=[
            pltpu.VMEM((n, rows, features // n), jnp.bfloat16),
            pltpu.VMEM((n, rows, LANES), jnp.bfloat16),
            pltpu.VMEM((n, rows, total), jnp.bfloat16),
            pltpu.VMEM((n, rows, total), jnp.bfloat16),
            pltpu.VMEM((n, rows, LANES), jnp.bfloat16),
            pltpu.VMEM((rows, width), jnp.bfloat16),
            pltpu.VMEM((1, rows), jnp.bfloat16),
            pltpu.VMEM((rows, features), jnp.bfloat16),
            pltpu.SemaphoreType.DMA((4,)),
            pltpu.SemaphoreType.DMA((4,)),
            pltpu.SemaphoreType.DMA((4,)),
        ],
        compiler_params=pltpu.CompilerParams(
            collective_id=0, has_side_effects=True, vmem_limit_bytes=32 * 1024 * 1024
        ),
        cost_estimate=pl.CostEstimate(
            flops=2 * total * total * (features // n),
            bytes_accessed=2 * rows * features,
            transcendentals=rows * total,
        ),
    )(*(pltpu.with_memory_space_constraint(x, pltpu.HBM) for x in operands))


def solution(mesh):
    placed = (P(("groups", "blk"), None), P(("groups", "blk"), None), P(("groups", "blk")))
    return jax.shard_map(
        functools.partial(shards, mesh.shape["blk"]),
        mesh=mesh,
        in_specs=placed,
        out_specs=(P(("groups", "blk"), None), P("groups", None)),
        check_vma=False,
    )
```

```python
import functools

import jax
import jax.numpy as jnp
from jax import lax
from jax.experimental import pallas as pl
from jax.experimental.pallas import tpu as pltpu
from jax.sharding import PartitionSpec as P

LANES = 128


def partners(me, n):
    half = n // 2
    upper = me >= half
    place = jnp.where(upper, me - half, me)
    mine = jnp.where(upper, half, 0)
    turned = [place] + [
        jnp.where(place >= half - j, place + j - half, place + j) for j in range(1, half)
    ]
    return [half - mine + t for t in turned] + [mine + t for t in turned[1:]]


def farthest_first(me, n):
    fours = n // 4
    four, place = me // 4, lax.rem(me, 4)
    turned = [jnp.where(place >= 4 - j, place + j - 4, place + j) for j in range(4)]
    upper = 2 * four >= fours
    beyond = jnp.where(upper, four, fours - 1 - four)
    order = []
    for k in range(fours - 1):
        outer = k < beyond
        ahead = jnp.where(outer, fours - 1 - k, k - beyond)
        behind = jnp.where(outer, k, fours - 1 - k + beyond)
        first = 4 * jnp.where(upper, behind, ahead)
        order += [first + t for t in turned]
    return order + [4 * four + t for t in turned[1:]]


def alternate(others):
    half = (len(others) + 1) // 2
    far, near = others[:half], others[half:]
    return [pick for pair in zip(far, near) for pick in pair] + [far[-1]]


def kernel(
    n,
    frames_ref,
    basis_ref,
    density_ref,
    residual_ref,
    coef_ref,
    gathered,
    aux,
    partial,
    arrived,
    applied,
    basis_vmem,
    density_vmem,
    staged,
    own_sem,
    send_sem,
    recv_sem,
):
    me = lax.axis_index("blk")
    rows, features = frames_ref.shape
    width = basis_ref.shape[1]
    span = features // n
    total = n * rows
    others = partners(me, n)
    by_distance = farthest_first(me, n)

    barrier = pltpu.get_barrier_semaphore()
    for other in by_distance:
        pl.semaphore_signal(
            barrier, inc=1, device_id={"blk": other}, device_id_type=pl.DeviceIdType.MESH
        )

    stage = pltpu.make_async_copy(frames_ref, staged, own_sem.at[0])
    stage.start()
    fetch_basis = pltpu.make_async_copy(basis_ref, basis_vmem, own_sem.at[1])
    fetch_basis.start()
    fetch_density = pltpu.make_async_copy(density_ref, density_vmem, own_sem.at[2])
    fetch_density.start()

    pl.semaphore_wait(barrier, n - 1)

    def send(src, dst, slot, other):
        pltpu.make_async_remote_copy(
            src_ref=src,
            dst_ref=dst,
            send_sem=send_sem.at[slot],
            recv_sem=recv_sem.at[slot],
            device_id={"blk": other},
            device_id_type=pl.DeviceIdType.MESH,
        ).start()

    def wait_all(buffer, sem):
        part = buffer.at[pl.ds(0, n - 1)]
        pltpu.make_async_copy(part, part, sem).wait()

    stage.wait()
    for other in alternate(others):
        send(
            staged.at[:, pl.ds(pl.multiple_of(other * span, span), span)],
            gathered.at[me],
            0,
            other,
        )
    own = pltpu.make_async_copy(
        staged.at[:, pl.ds(pl.multiple_of(me * span, span), span)], gathered.at[me], own_sem.at[3]
    )
    own.start()

    own_frames = staged[...].astype(jnp.float32)
    own_norms = jnp.sum(own_frames * own_frames, axis=1, keepdims=True)
    norm_parts = []
    rest = own_norms
    for _ in range(3):
        norm_parts.append(rest.astype(jnp.bfloat16).astype(jnp.float32))
        rest = rest - norm_parts[-1]

    row_id = lax.broadcasted_iota(jnp.int32, (rows, rows), 0)
    col_id = lax.broadcasted_iota(jnp.int32, (rows, rows), 1)
    fetch_density.wait()
    density_row = density_vmem[...].astype(jnp.float32)
    density_col = jnp.sum(
        jnp.where(row_id == col_id, jnp.broadcast_to(density_row, (rows, rows)), 0.0),
        axis=1,
        keepdims=True,
    )
    fetch_basis.wait()
    own_basis = basis_vmem[...].astype(jnp.float32)
    lane = lax.broadcasted_iota(jnp.int32, (rows, LANES), 1)
    own_wide = jnp.concatenate(
        [own_basis, jnp.broadcast_to(density_col, (rows, LANES - width))], axis=1
    )
    for index, part in enumerate(norm_parts):
        own_wide = jnp.where(lane == width + 1 + index, part, own_wide)
    aux[me] = own_wide.astype(jnp.bfloat16)
    for other in by_distance:
        send(aux.at[me], aux.at[me], 1, other)

    eye = lax.broadcasted_iota(jnp.int32, (total, total), 0) == lax.broadcasted_iota(
        jnp.int32, (total, total), 1
    )
    own.wait()
    wait_all(gathered, recv_sem.at[0])
    block = gathered[...].reshape(total, span)
    gram = lax.dot_general(
        block, block, (((1,), (1,)), ((), ())), preferred_element_type=jnp.float32
    )
    partial[...] = gram.reshape(n, rows, total)
    for other in by_distance:
        send(partial.at[other], arrived.at[me], 2, other)
    arrived[me] = partial[me]

    wait_all(aux, recv_sem.at[1])
    wide = aux[...].astype(jnp.float32).reshape(total, LANES)
    density_all = jnp.sum(jnp.where(eye, wide[:, width : width + 1], 0.0), axis=0, keepdims=True)
    norms = sum(wide[:, width + 1 + index : width + 2 + index] for index in range(3))
    norm_sums = own_norms + jnp.sum(jnp.where(eye, norms, 0.0), axis=0, keepdims=True)
    vectors = wide[:, :width]
    twice = jnp.concatenate([vectors, vectors], axis=1).astype(jnp.bfloat16)

    wait_all(arrived, recv_sem.at[2])

    squared_dist = norm_sums - 2.0 * jnp.sum(arrived[...], axis=0)
    weight = (jnp.exp(squared_dist * (-1.0 / features)) * density_all).astype(jnp.bfloat16)
    numer = jnp.dot(weight, twice, preferred_element_type=jnp.float32)
    totals = jnp.sum(weight.astype(jnp.float32), axis=1, keepdims=True)
    own_applied = numer / totals
    high = own_applied.astype(jnp.bfloat16).astype(jnp.float32)
    applied[me] = jnp.where(lane < width, high, own_applied - high).astype(jnp.bfloat16)
    for other in by_distance:
        send(applied.at[me], applied.at[me], 3, other)

    overlap = lax.dot_general(
        own_basis.astype(jnp.bfloat16),
        vectors.astype(jnp.bfloat16),
        (((1,), (1,)), ((), ())),
        preferred_element_type=jnp.float32,
    )
    overlap_high = overlap.astype(jnp.bfloat16).astype(jnp.float32)
    onto = jnp.concatenate(
        [jnp.transpose(wide)[:width], overlap_high, overlap - overlap_high], axis=0
    ).astype(jnp.bfloat16)

    wait_all(applied, recv_sem.at[3])

    products = jnp.dot(
        onto, applied[...].reshape(total, LANES), preferred_element_type=jnp.float32
    )
    products = products[:, :width] + products[:, width : 2 * width]
    coef_ref[...] = products[:width]
    projection = products[width : width + rows] + products[width + rows :]
    residual_ref[...] = (own_applied[:, :width] - projection * (1.0 / total)).astype(jnp.bfloat16)

    wait_all(gathered, send_sem.at[0])
    wait_all(aux, send_sem.at[1])
    wait_all(arrived, send_sem.at[2])
    wait_all(applied, send_sem.at[3])


def shards(n, frames, basis, density):
    rows, features = frames.shape
    width = basis.shape[1]
    total = n * rows
    vmem = pl.BlockSpec(memory_space=pltpu.VMEM)
    operands = (frames, basis, density.reshape(1, rows))
    return pl.pallas_call(
        functools.partial(kernel, n),
        out_shape=(
            jax.ShapeDtypeStruct((rows, width), jnp.bfloat16),
            jax.ShapeDtypeStruct((width, width), jnp.float32),
        ),
        in_specs=[pl.BlockSpec(memory_space=pltpu.HBM)] * 3,
        out_specs=(vmem, vmem),
        scratch_shapes=[
            pltpu.VMEM((n, rows, features // n), jnp.bfloat16),
            pltpu.VMEM((n, rows, LANES), jnp.bfloat16),
            pltpu.VMEM((n, rows, total), jnp.float32),
            pltpu.VMEM((n, rows, total), jnp.float32),
            pltpu.VMEM((n, rows, LANES), jnp.bfloat16),
            pltpu.VMEM((rows, width), jnp.bfloat16),
            pltpu.VMEM((1, rows), jnp.bfloat16),
            pltpu.VMEM((rows, features), jnp.bfloat16),
            pltpu.SemaphoreType.DMA((4,)),
            pltpu.SemaphoreType.DMA((4,)),
            pltpu.SemaphoreType.DMA((4,)),
        ],
        compiler_params=pltpu.CompilerParams(
            collective_id=0, has_side_effects=True, vmem_limit_bytes=32 * 1024 * 1024
        ),
        cost_estimate=pl.CostEstimate(
            flops=2 * total * total * (features // n),
            bytes_accessed=2 * rows * features,
            transcendentals=rows * total,
        ),
    )(*(pltpu.with_memory_space_constraint(x, pltpu.HBM) for x in operands))


def solution(mesh):
    placed = (P(("groups", "blk"), None), P(("groups", "blk"), None), P(("groups", "blk")))
    return jax.shard_map(
        functools.partial(shards, mesh.shape["blk"]),
        mesh=mesh,
        in_specs=placed,
        out_specs=(P(("groups", "blk"), None), P("groups", None)),
        check_vma=False,
    )
```

```python
import functools

import jax
import jax.numpy as jnp
from jax import lax
from jax.experimental import pallas as pl
from jax.experimental.pallas import tpu as pltpu
from jax.sharding import PartitionSpec as P

LANES = 128


def partners(me, n):
    half = n // 2
    upper = me >= half
    place = jnp.where(upper, me - half, me)
    mine = jnp.where(upper, half, 0)
    turned = [place] + [
        jnp.where(place >= half - j, place + j - half, place + j) for j in range(1, half)
    ]
    return [half - mine + t for t in turned] + [mine + t for t in turned[1:]]


def farthest_first(me, n):
    fours = n // 4
    four, place = me // 4, lax.rem(me, 4)
    turned = [jnp.where(place >= 4 - j, place + j - 4, place + j) for j in range(4)]
    upper = 2 * four >= fours
    beyond = jnp.where(upper, four, fours - 1 - four)
    order = []
    for k in range(fours - 1):
        outer = k < beyond
        ahead = jnp.where(outer, fours - 1 - k, k - beyond)
        behind = jnp.where(outer, k, fours - 1 - k + beyond)
        first = 4 * jnp.where(upper, behind, ahead)
        order += [first + t for t in turned]
    return order + [4 * four + t for t in turned[1:]]


def alternate(others):
    half = (len(others) + 1) // 2
    far, near = others[:half], others[half:]
    return [pick for pair in zip(far, near) for pick in pair] + [far[-1]]


def kernel(
    n,
    frames_ref,
    basis_ref,
    density_ref,
    residual_ref,
    coef_ref,
    gathered,
    aux,
    partial,
    arrived,
    applied,
    basis_vmem,
    density_vmem,
    staged,
    own_sem,
    send_sem,
    recv_sem,
):
    me = lax.axis_index("blk")
    rows, features = frames_ref.shape
    width = basis_ref.shape[1]
    span = features // n
    total = n * rows
    others = partners(me, n)
    by_distance = farthest_first(me, n)

    barrier = pltpu.get_barrier_semaphore()
    for other in by_distance:
        pl.semaphore_signal(
            barrier, inc=1, device_id={"blk": other}, device_id_type=pl.DeviceIdType.MESH
        )

    stage = pltpu.make_async_copy(frames_ref, staged, own_sem.at[0])
    stage.start()
    fetch_basis = pltpu.make_async_copy(basis_ref, basis_vmem, own_sem.at[1])
    fetch_basis.start()
    fetch_density = pltpu.make_async_copy(density_ref, density_vmem, own_sem.at[2])
    fetch_density.start()

    pl.semaphore_wait(barrier, n - 1)

    def send(src, dst, slot, other):
        pltpu.make_async_remote_copy(
            src_ref=src,
            dst_ref=dst,
            send_sem=send_sem.at[slot],
            recv_sem=recv_sem.at[slot],
            device_id={"blk": other},
            device_id_type=pl.DeviceIdType.MESH,
        ).start()

    def wait_all(buffer, sem):
        part = buffer.at[pl.ds(0, n - 1)]
        pltpu.make_async_copy(part, part, sem).wait()

    stage.wait()
    for other in alternate(others):
        send(
            staged.at[:, pl.ds(pl.multiple_of(other * span, span), span)],
            gathered.at[me],
            0,
            other,
        )
    own = pltpu.make_async_copy(
        staged.at[:, pl.ds(pl.multiple_of(me * span, span), span)], gathered.at[me], own_sem.at[3]
    )
    own.start()

    own_frames = staged[...].astype(jnp.float32)
    own_norms = jnp.sum(own_frames * own_frames, axis=1, keepdims=True)
    norm_parts = []
    rest = own_norms
    for _ in range(3):
        norm_parts.append(rest.astype(jnp.bfloat16).astype(jnp.float32))
        rest = rest - norm_parts[-1]

    row_id = lax.broadcasted_iota(jnp.int32, (rows, rows), 0)
    col_id = lax.broadcasted_iota(jnp.int32, (rows, rows), 1)
    fetch_density.wait()
    density_row = density_vmem[...].astype(jnp.float32)
    density_col = jnp.sum(
        jnp.where(row_id == col_id, jnp.broadcast_to(density_row, (rows, rows)), 0.0),
        axis=1,
        keepdims=True,
    )
    fetch_basis.wait()
    own_basis = basis_vmem[...].astype(jnp.float32)
    lane = lax.broadcasted_iota(jnp.int32, (rows, LANES), 1)
    own_wide = jnp.concatenate(
        [own_basis, jnp.broadcast_to(density_col, (rows, LANES - width))], axis=1
    )
    for index, part in enumerate(norm_parts):
        own_wide = jnp.where(lane == width + 1 + index, part, own_wide)
    aux[me] = own_wide.astype(jnp.bfloat16)
    for other in by_distance:
        send(aux.at[me], aux.at[me], 1, other)

    eye = lax.broadcasted_iota(jnp.int32, (total, total), 0) == lax.broadcasted_iota(
        jnp.int32, (total, total), 1
    )
    own.wait()
    wait_all(gathered, recv_sem.at[0])
    block = gathered[...].reshape(total, span)
    gram = lax.dot_general(
        block, block, (((1,), (1,)), ((), ())), preferred_element_type=jnp.float32
    )
    partial[...] = gram.reshape(n, rows, total)
    for other in by_distance:
        send(partial.at[other], arrived.at[me], 2, other)
    arrived[me] = partial[me]

    wait_all(aux, recv_sem.at[1])
    wide = aux[...].astype(jnp.float32).reshape(total, LANES)
    density_all = jnp.sum(jnp.where(eye, wide[:, width : width + 1], 0.0), axis=0, keepdims=True)
    norms = sum(wide[:, width + 1 + index : width + 2 + index] for index in range(3))
    norm_sums = own_norms + jnp.sum(jnp.where(eye, norms, 0.0), axis=0, keepdims=True)
    vectors = wide[:, :width]
    twice = jnp.concatenate([vectors, vectors], axis=1).astype(jnp.bfloat16)

    wait_all(arrived, recv_sem.at[2])

    squared_dist = norm_sums - 2.0 * jnp.sum(arrived[...], axis=0)
    weight = (jnp.exp(squared_dist * (-1.0 / features)) * density_all).astype(jnp.bfloat16)
    numer = jnp.dot(weight, twice, preferred_element_type=jnp.float32)
    totals = jnp.sum(weight.astype(jnp.float32), axis=1, keepdims=True)
    own_applied = numer / totals
    high = own_applied.astype(jnp.bfloat16).astype(jnp.float32)
    applied[me] = jnp.where(lane < width, high, own_applied - high).astype(jnp.bfloat16)
    for other in by_distance:
        send(applied.at[me], applied.at[me], 3, other)

    overlap = lax.dot_general(
        own_basis.astype(jnp.bfloat16),
        vectors.astype(jnp.bfloat16),
        (((1,), (1,)), ((), ())),
        preferred_element_type=jnp.float32,
    )
    overlap_high = overlap.astype(jnp.bfloat16).astype(jnp.float32)
    onto = jnp.concatenate(
        [jnp.transpose(wide)[:width], overlap_high, overlap - overlap_high], axis=0
    ).astype(jnp.bfloat16)

    wait_all(applied, recv_sem.at[3])

    products = jnp.dot(
        onto, applied[...].reshape(total, LANES), preferred_element_type=jnp.float32
    )
    products = products[:, :width] + products[:, width : 2 * width]
    coef_ref[...] = products[:width]
    projection = products[width : width + rows] + products[width + rows :]
    residual_ref[...] = (own_applied[:, :width] - projection * (1.0 / total)).astype(jnp.bfloat16)

    wait_all(gathered, send_sem.at[0])
    wait_all(aux, send_sem.at[1])
    wait_all(arrived, send_sem.at[2])
    wait_all(applied, send_sem.at[3])


def deliver(residual_vmem, coef_vmem, residual_ref, coef_ref, sem):
    copies = [
        pltpu.make_async_copy(coef_vmem, coef_ref, sem.at[0]),
        pltpu.make_async_copy(residual_vmem, residual_ref, sem.at[1]),
    ]
    for copy in copies:
        copy.start()
    for copy in copies:
        copy.wait()


def shards(n, frames, basis, density):
    rows, features = frames.shape
    width = basis.shape[1]
    total = n * rows
    vmem = pl.BlockSpec(memory_space=pltpu.VMEM)
    operands = (frames, basis, density.reshape(1, rows))
    out_shape = (
        jax.ShapeDtypeStruct((rows, width), jnp.bfloat16),
        jax.ShapeDtypeStruct((width, width), jnp.float32),
    )
    results = pl.pallas_call(
        functools.partial(kernel, n),
        out_shape=out_shape,
        in_specs=[pl.BlockSpec(memory_space=pltpu.HBM)] * 3,
        out_specs=(vmem, vmem),
        scratch_shapes=[
            pltpu.VMEM((n, rows, features // n), jnp.bfloat16),
            pltpu.VMEM((n, rows, LANES), jnp.bfloat16),
            pltpu.VMEM((n, rows, total), jnp.float32),
            pltpu.VMEM((n, rows, total), jnp.float32),
            pltpu.VMEM((n, rows, LANES), jnp.bfloat16),
            pltpu.VMEM((rows, width), jnp.bfloat16),
            pltpu.VMEM((1, rows), jnp.bfloat16),
            pltpu.VMEM((rows, features), jnp.bfloat16),
            pltpu.SemaphoreType.DMA((4,)),
            pltpu.SemaphoreType.DMA((4,)),
            pltpu.SemaphoreType.DMA((4,)),
        ],
        compiler_params=pltpu.CompilerParams(
            collective_id=0, has_side_effects=True, vmem_limit_bytes=32 * 1024 * 1024
        ),
        cost_estimate=pl.CostEstimate(
            flops=2 * total * total * (features // n),
            bytes_accessed=2 * rows * features,
            transcendentals=rows * total,
        ),
    )(*(pltpu.with_memory_space_constraint(x, pltpu.HBM) for x in operands))
    return pl.pallas_call(
        deliver,
        out_shape=out_shape,
        in_specs=[vmem, vmem],
        out_specs=(pl.BlockSpec(memory_space=pltpu.HBM),) * 2,
        scratch_shapes=[pltpu.SemaphoreType.DMA((2,))],
        compiler_params=pltpu.CompilerParams(vmem_limit_bytes=1024 * 1024),
    )(*(pltpu.with_memory_space_constraint(x, pltpu.VMEM) for x in results))


def solution(mesh):
    placed = (P(("groups", "blk"), None), P(("groups", "blk"), None), P(("groups", "blk")))
    return jax.shard_map(
        functools.partial(shards, mesh.shape["blk"]),
        mesh=mesh,
        in_specs=placed,
        out_specs=(P(("groups", "blk"), None), P("groups", None)),
        check_vma=False,
    )
```

```python
import functools

import jax
import jax.numpy as jnp
from jax import lax
from jax.experimental import pallas as pl
from jax.experimental.pallas import tpu as pltpu
from jax.sharding import PartitionSpec as P

LANES = 128


def farthest_first(me, n):
    fours = n // 4
    four, place = me // 4, lax.rem(me, 4)
    turned = [jnp.where(place >= 4 - j, place + j - 4, place + j) for j in range(4)]
    upper = 2 * four >= fours
    beyond = jnp.where(upper, four, fours - 1 - four)
    order = []
    for k in range(fours - 1):
        outer = k < beyond
        ahead = jnp.where(outer, fours - 1 - k, k - beyond)
        behind = jnp.where(outer, k, fours - 1 - k + beyond)
        first = 4 * jnp.where(upper, behind, ahead)
        order += [first + t for t in turned]
    return order + [4 * four + t for t in turned[1:]]


def kernel(
    n,
    frames_ref,
    basis_ref,
    density_ref,
    residual_ref,
    coef_ref,
    gathered,
    aux,
    partial,
    arrived,
    applied,
    basis_vmem,
    density_vmem,
    staged,
    own_sem,
    send_sem,
    recv_sem,
):
    me = lax.axis_index("blk")
    rows, features = frames_ref.shape
    width = basis_ref.shape[1]
    span = features // n
    total = n * rows
    others = farthest_first(me, n)

    barrier = pltpu.get_barrier_semaphore()
    for other in others:
        pl.semaphore_signal(
            barrier, inc=1, device_id={"blk": other}, device_id_type=pl.DeviceIdType.MESH
        )

    stage = pltpu.make_async_copy(frames_ref, staged, own_sem.at[0])
    stage.start()
    fetch_basis = pltpu.make_async_copy(basis_ref, basis_vmem, own_sem.at[1])
    fetch_basis.start()
    fetch_density = pltpu.make_async_copy(density_ref, density_vmem, own_sem.at[2])
    fetch_density.start()

    pl.semaphore_wait(barrier, n - 1)

    def send(src, dst, slot, other):
        pltpu.make_async_remote_copy(
            src_ref=src,
            dst_ref=dst,
            send_sem=send_sem.at[slot],
            recv_sem=recv_sem.at[slot],
            device_id={"blk": other},
            device_id_type=pl.DeviceIdType.MESH,
        ).start()

    def wait_all(buffer, sem):
        part = buffer.at[pl.ds(0, n - 1)]
        pltpu.make_async_copy(part, part, sem).wait()

    stage.wait()
    for other in others:
        send(
            staged.at[:, pl.ds(pl.multiple_of(other * span, span), span)],
            gathered.at[me],
            0,
            other,
        )
    own = pltpu.make_async_copy(
        staged.at[:, pl.ds(pl.multiple_of(me * span, span), span)], gathered.at[me], own_sem.at[3]
    )
    own.start()

    own_frames = staged[...].astype(jnp.float32)
    own_norms = jnp.sum(own_frames * own_frames, axis=1, keepdims=True)
    norm_parts = []
    rest = own_norms
    for _ in range(3):
        norm_parts.append(rest.astype(jnp.bfloat16).astype(jnp.float32))
        rest = rest - norm_parts[-1]

    row_id = lax.broadcasted_iota(jnp.int32, (rows, rows), 0)
    col_id = lax.broadcasted_iota(jnp.int32, (rows, rows), 1)
    fetch_density.wait()
    density_row = density_vmem[...].astype(jnp.float32)
    density_col = jnp.sum(
        jnp.where(row_id == col_id, jnp.broadcast_to(density_row, (rows, rows)), 0.0),
        axis=1,
        keepdims=True,
    )
    fetch_basis.wait()
    own_basis = basis_vmem[...].astype(jnp.float32)
    lane = lax.broadcasted_iota(jnp.int32, (rows, LANES), 1)
    own_wide = jnp.concatenate(
        [own_basis, jnp.broadcast_to(density_col, (rows, LANES - width))], axis=1
    )
    for index, part in enumerate(norm_parts):
        own_wide = jnp.where(lane == width + 1 + index, part, own_wide)
    aux[me] = own_wide.astype(jnp.bfloat16)
    for other in others:
        send(aux.at[me], aux.at[me], 1, other)

    eye = lax.broadcasted_iota(jnp.int32, (total, total), 0) == lax.broadcasted_iota(
        jnp.int32, (total, total), 1
    )
    own.wait()
    wait_all(gathered, recv_sem.at[0])
    block = gathered[...].reshape(total, span)
    gram = lax.dot_general(
        block, block, (((1,), (1,)), ((), ())), preferred_element_type=jnp.float32
    )
    partial[...] = gram.reshape(n, rows, total)
    for other in others:
        send(partial.at[other], arrived.at[me], 2, other)
    arrived[me] = partial[me]

    wait_all(aux, recv_sem.at[1])
    wide = aux[...].astype(jnp.float32).reshape(total, LANES)
    density_all = jnp.sum(jnp.where(eye, wide[:, width : width + 1], 0.0), axis=0, keepdims=True)
    norms = sum(wide[:, width + 1 + index : width + 2 + index] for index in range(3))
    norm_sums = own_norms + jnp.sum(jnp.where(eye, norms, 0.0), axis=0, keepdims=True)
    vectors = wide[:, :width]
    twice = jnp.concatenate([vectors, vectors], axis=1).astype(jnp.bfloat16)

    wait_all(arrived, recv_sem.at[2])

    squared_dist = norm_sums - 2.0 * jnp.sum(arrived[...], axis=0)
    weight = (jnp.exp(squared_dist * (-1.0 / features)) * density_all).astype(jnp.bfloat16)
    numer = jnp.dot(weight, twice, preferred_element_type=jnp.float32)
    totals = jnp.sum(weight.astype(jnp.float32), axis=1, keepdims=True)
    own_applied = numer / totals
    high = own_applied.astype(jnp.bfloat16).astype(jnp.float32)
    applied[me] = jnp.where(lane < width, high, own_applied - high).astype(jnp.bfloat16)
    for other in others:
        send(applied.at[me], applied.at[me], 3, other)

    overlap = lax.dot_general(
        own_basis.astype(jnp.bfloat16),
        vectors.astype(jnp.bfloat16),
        (((1,), (1,)), ((), ())),
        preferred_element_type=jnp.float32,
    )
    overlap_high = overlap.astype(jnp.bfloat16).astype(jnp.float32)
    onto = jnp.concatenate(
        [jnp.transpose(wide)[:width], overlap_high, overlap - overlap_high], axis=0
    ).astype(jnp.bfloat16)

    wait_all(applied, recv_sem.at[3])

    products = jnp.dot(
        onto, applied[...].reshape(total, LANES), preferred_element_type=jnp.float32
    )
    products = products[:, :width] + products[:, width : 2 * width]
    coef_ref[...] = products[:width]
    projection = products[width : width + rows] + products[width + rows :]
    residual_ref[...] = (own_applied[:, :width] - projection * (1.0 / total)).astype(jnp.bfloat16)

    wait_all(gathered, send_sem.at[0])
    wait_all(aux, send_sem.at[1])
    wait_all(arrived, send_sem.at[2])
    wait_all(applied, send_sem.at[3])


def deliver(residual_vmem, coef_vmem, residual_ref, coef_ref, sem):
    copies = [
        pltpu.make_async_copy(coef_vmem, coef_ref, sem.at[0]),
        pltpu.make_async_copy(residual_vmem, residual_ref, sem.at[1]),
    ]
    for copy in copies:
        copy.start()
    for copy in copies:
        copy.wait()


def shards(n, frames, basis, density):
    rows, features = frames.shape
    width = basis.shape[1]
    total = n * rows
    vmem = pl.BlockSpec(memory_space=pltpu.VMEM)
    operands = (frames, basis, density.reshape(1, rows))
    out_shape = (
        jax.ShapeDtypeStruct((rows, width), jnp.bfloat16),
        jax.ShapeDtypeStruct((width, width), jnp.float32),
    )
    results = pl.pallas_call(
        functools.partial(kernel, n),
        out_shape=out_shape,
        in_specs=[pl.BlockSpec(memory_space=pltpu.HBM)] * 3,
        out_specs=(vmem, vmem),
        scratch_shapes=[
            pltpu.VMEM((n, rows, features // n), jnp.bfloat16),
            pltpu.VMEM((n, rows, LANES), jnp.bfloat16),
            pltpu.VMEM((n, rows, total), jnp.float32),
            pltpu.VMEM((n, rows, total), jnp.float32),
            pltpu.VMEM((n, rows, LANES), jnp.bfloat16),
            pltpu.VMEM((rows, width), jnp.bfloat16),
            pltpu.VMEM((1, rows), jnp.bfloat16),
            pltpu.VMEM((rows, features), jnp.bfloat16),
            pltpu.SemaphoreType.DMA((4,)),
            pltpu.SemaphoreType.DMA((4,)),
            pltpu.SemaphoreType.DMA((4,)),
        ],
        compiler_params=pltpu.CompilerParams(
            collective_id=0, has_side_effects=True, vmem_limit_bytes=32 * 1024 * 1024
        ),
        cost_estimate=pl.CostEstimate(
            flops=2 * total * total * (features // n),
            bytes_accessed=2 * rows * features,
            transcendentals=rows * total,
        ),
    )(*(pltpu.with_memory_space_constraint(x, pltpu.HBM) for x in operands))
    return pl.pallas_call(
        deliver,
        out_shape=out_shape,
        in_specs=[vmem, vmem],
        out_specs=(pl.BlockSpec(memory_space=pltpu.HBM),) * 2,
        scratch_shapes=[pltpu.SemaphoreType.DMA((2,))],
        compiler_params=pltpu.CompilerParams(vmem_limit_bytes=1024 * 1024),
    )(*(pltpu.with_memory_space_constraint(x, pltpu.VMEM) for x in results))


def solution(mesh):
    placed = (P(("groups", "blk"), None), P(("groups", "blk"), None), P(("groups", "blk")))
    return jax.shard_map(
        functools.partial(shards, mesh.shape["blk"]),
        mesh=mesh,
        in_specs=placed,
        out_specs=(P(("groups", "blk"), None), P("groups", None)),
        check_vma=False,
    )
```

```python
import functools

import jax
import jax.numpy as jnp
from jax import lax
from jax.experimental import pallas as pl
from jax.experimental.pallas import tpu as pltpu
from jax.sharding import PartitionSpec as P

LANES = 128


def farthest_first(me, n):
    fours = n // 4
    four, place = me // 4, lax.rem(me, 4)
    turned = [jnp.where(place >= 4 - j, place + j - 4, place + j) for j in range(4)]
    upper = 2 * four >= fours
    beyond = jnp.where(upper, four, fours - 1 - four)
    order = []
    for k in range(fours - 1):
        outer = k < beyond
        ahead = jnp.where(outer, fours - 1 - k, k - beyond)
        behind = jnp.where(outer, k, fours - 1 - k + beyond)
        first = 4 * jnp.where(upper, behind, ahead)
        order += [first + t for t in turned]
    return order + [4 * four + t for t in turned[1:]]


def kernel(
    n,
    frames_ref,
    basis_ref,
    density_ref,
    residual_ref,
    coef_ref,
    gathered,
    aux,
    partial,
    arrived,
    applied,
    basis_vmem,
    density_vmem,
    staged,
    own_sem,
    send_sem,
    recv_sem,
):
    me = lax.axis_index("blk")
    rows, features = frames_ref.shape
    width = basis_ref.shape[1]
    span = features // n
    total = n * rows
    others = farthest_first(me, n)

    barrier = pltpu.get_barrier_semaphore()
    for other in others:
        pl.semaphore_signal(
            barrier, inc=1, device_id={"blk": other}, device_id_type=pl.DeviceIdType.MESH
        )

    stage = pltpu.make_async_copy(frames_ref, staged, own_sem.at[0])
    stage.start()
    fetch_basis = pltpu.make_async_copy(basis_ref, basis_vmem, own_sem.at[1])
    fetch_basis.start()
    fetch_density = pltpu.make_async_copy(density_ref, density_vmem, own_sem.at[2])
    fetch_density.start()

    pl.semaphore_wait(barrier, n - 1)

    def send(src, dst, slot, other):
        pltpu.make_async_remote_copy(
            src_ref=src,
            dst_ref=dst,
            send_sem=send_sem.at[slot],
            recv_sem=recv_sem.at[slot],
            device_id={"blk": other},
            device_id_type=pl.DeviceIdType.MESH,
        ).start()

    def wait_all(buffer, sem):
        part = buffer.at[pl.ds(0, n - 1)]
        pltpu.make_async_copy(part, part, sem).wait()

    stage.wait()
    for other in others:
        send(
            staged.at[:, pl.ds(pl.multiple_of(other * span, span), span)],
            gathered.at[me],
            0,
            other,
        )
    own = pltpu.make_async_copy(
        staged.at[:, pl.ds(pl.multiple_of(me * span, span), span)], gathered.at[me], own_sem.at[3]
    )
    own.start()

    own_frames = staged[...].astype(jnp.float32)
    own_norms = jnp.sum(own_frames * own_frames, axis=1, keepdims=True)
    norm_parts = []
    rest = own_norms
    for _ in range(3):
        norm_parts.append(rest.astype(jnp.bfloat16).astype(jnp.float32))
        rest = rest - norm_parts[-1]

    row_id = lax.broadcasted_iota(jnp.int32, (rows, rows), 0)
    col_id = lax.broadcasted_iota(jnp.int32, (rows, rows), 1)
    fetch_density.wait()
    density_row = density_vmem[...].astype(jnp.float32)
    density_col = jnp.sum(
        jnp.where(row_id == col_id, jnp.broadcast_to(density_row, (rows, rows)), 0.0),
        axis=1,
        keepdims=True,
    )
    fetch_basis.wait()
    own_basis = basis_vmem[...].astype(jnp.float32)
    lane = lax.broadcasted_iota(jnp.int32, (rows, LANES), 1)
    own_wide = jnp.concatenate(
        [own_basis, jnp.broadcast_to(density_col, (rows, LANES - width))], axis=1
    )
    for index, part in enumerate(norm_parts):
        own_wide = jnp.where(lane == width + 1 + index, part, own_wide)
    aux[me] = own_wide.astype(jnp.bfloat16)
    wait_all(gathered, send_sem.at[0])
    for other in others:
        send(aux.at[me], aux.at[me], 1, other)

    eye = lax.broadcasted_iota(jnp.int32, (total, total), 0) == lax.broadcasted_iota(
        jnp.int32, (total, total), 1
    )
    own.wait()
    wait_all(gathered, recv_sem.at[0])
    block = gathered[...].reshape(total, span)
    gram = lax.dot_general(
        block, block, (((1,), (1,)), ((), ())), preferred_element_type=jnp.float32
    )
    partial[...] = gram.reshape(n, rows, total)
    for other in others:
        send(partial.at[other], arrived.at[me], 2, other)
    arrived[me] = partial[me]

    wait_all(aux, recv_sem.at[1])
    wide = aux[...].astype(jnp.float32).reshape(total, LANES)
    density_all = jnp.sum(jnp.where(eye, wide[:, width : width + 1], 0.0), axis=0, keepdims=True)
    norms = sum(wide[:, width + 1 + index : width + 2 + index] for index in range(3))
    norm_sums = own_norms + jnp.sum(jnp.where(eye, norms, 0.0), axis=0, keepdims=True)
    vectors = wide[:, :width]
    twice = jnp.concatenate([vectors, vectors], axis=1).astype(jnp.bfloat16)

    wait_all(arrived, recv_sem.at[2])

    squared_dist = norm_sums - 2.0 * jnp.sum(arrived[...], axis=0)
    weight = (jnp.exp(squared_dist * (-1.0 / features)) * density_all).astype(jnp.bfloat16)
    numer = jnp.dot(weight, twice, preferred_element_type=jnp.float32)
    totals = jnp.sum(weight.astype(jnp.float32), axis=1, keepdims=True)
    own_applied = numer / totals
    high = own_applied.astype(jnp.bfloat16).astype(jnp.float32)
    applied[me] = jnp.where(lane < width, high, own_applied - high).astype(jnp.bfloat16)
    for other in others:
        send(applied.at[me], applied.at[me], 3, other)

    overlap = lax.dot_general(
        own_basis.astype(jnp.bfloat16),
        vectors.astype(jnp.bfloat16),
        (((1,), (1,)), ((), ())),
        preferred_element_type=jnp.float32,
    )
    overlap_high = overlap.astype(jnp.bfloat16).astype(jnp.float32)
    onto = jnp.concatenate(
        [jnp.transpose(wide)[:width], overlap_high, overlap - overlap_high], axis=0
    ).astype(jnp.bfloat16)

    wait_all(aux, send_sem.at[1])
    wait_all(arrived, send_sem.at[2])
    wait_all(applied, recv_sem.at[3])

    products = jnp.dot(
        onto, applied[...].reshape(total, LANES), preferred_element_type=jnp.float32
    )
    products = products[:, :width] + products[:, width : 2 * width]
    coef_ref[...] = products[:width]
    projection = products[width : width + rows] + products[width + rows :]
    residual_ref[...] = (own_applied[:, :width] - projection * (1.0 / total)).astype(jnp.bfloat16)

    wait_all(applied, send_sem.at[3])


def deliver(residual_vmem, coef_vmem, residual_ref, coef_ref, sem):
    copies = [
        pltpu.make_async_copy(coef_vmem, coef_ref, sem.at[0]),
        pltpu.make_async_copy(residual_vmem, residual_ref, sem.at[1]),
    ]
    for copy in copies:
        copy.start()
    for copy in copies:
        copy.wait()


def shards(n, frames, basis, density):
    rows, features = frames.shape
    width = basis.shape[1]
    total = n * rows
    vmem = pl.BlockSpec(memory_space=pltpu.VMEM)
    operands = (frames, basis, density.reshape(1, rows))
    out_shape = (
        jax.ShapeDtypeStruct((rows, width), jnp.bfloat16),
        jax.ShapeDtypeStruct((width, width), jnp.float32),
    )
    results = pl.pallas_call(
        functools.partial(kernel, n),
        out_shape=out_shape,
        in_specs=[pl.BlockSpec(memory_space=pltpu.HBM)] * 3,
        out_specs=(vmem, vmem),
        scratch_shapes=[
            pltpu.VMEM((n, rows, features // n), jnp.bfloat16),
            pltpu.VMEM((n, rows, LANES), jnp.bfloat16),
            pltpu.VMEM((n, rows, total), jnp.float32),
            pltpu.VMEM((n, rows, total), jnp.float32),
            pltpu.VMEM((n, rows, LANES), jnp.bfloat16),
            pltpu.VMEM((rows, width), jnp.bfloat16),
            pltpu.VMEM((1, rows), jnp.bfloat16),
            pltpu.VMEM((rows, features), jnp.bfloat16),
            pltpu.SemaphoreType.DMA((4,)),
            pltpu.SemaphoreType.DMA((4,)),
            pltpu.SemaphoreType.DMA((4,)),
        ],
        compiler_params=pltpu.CompilerParams(
            collective_id=0, has_side_effects=True, vmem_limit_bytes=32 * 1024 * 1024
        ),
        cost_estimate=pl.CostEstimate(
            flops=2 * total * total * (features // n),
            bytes_accessed=2 * rows * features,
            transcendentals=rows * total,
        ),
    )(*(pltpu.with_memory_space_constraint(x, pltpu.HBM) for x in operands))
    return pl.pallas_call(
        deliver,
        out_shape=out_shape,
        in_specs=[vmem, vmem],
        out_specs=(pl.BlockSpec(memory_space=pltpu.HBM),) * 2,
        scratch_shapes=[pltpu.SemaphoreType.DMA((2,))],
        compiler_params=pltpu.CompilerParams(vmem_limit_bytes=1024 * 1024),
    )(*(pltpu.with_memory_space_constraint(x, pltpu.VMEM) for x in results))


def solution(mesh):
    placed = (P(("groups", "blk"), None), P(("groups", "blk"), None), P(("groups", "blk")))
    return jax.shard_map(
        functools.partial(shards, mesh.shape["blk"]),
        mesh=mesh,
        in_specs=placed,
        out_specs=(P(("groups", "blk"), None), P("groups", None)),
        check_vma=False,
    )
```

```python
import functools

import jax
import jax.numpy as jnp
from jax import lax
from jax.experimental import pallas as pl
from jax.experimental.pallas import tpu as pltpu
from jax.sharding import PartitionSpec as P

LANES = 128


def farthest_first(me, n):
    fours = n // 4
    four, place = me // 4, lax.rem(me, 4)
    turned = [jnp.where(place >= 4 - j, place + j - 4, place + j) for j in range(4)]
    upper = 2 * four >= fours
    beyond = jnp.where(upper, four, fours - 1 - four)
    order = []
    for k in range(fours - 1):
        outer = k < beyond
        ahead = jnp.where(outer, fours - 1 - k, k - beyond)
        behind = jnp.where(outer, k, fours - 1 - k + beyond)
        first = 4 * jnp.where(upper, behind, ahead)
        order += [first + t for t in turned]
    return order + [4 * four + t for t in turned[1:]]


def kernel(
    n,
    frames_ref,
    basis_ref,
    density_ref,
    residual_ref,
    coef_ref,
    gathered,
    aux,
    partial,
    arrived,
    applied,
    basis_vmem,
    density_vmem,
    staged,
    own_sem,
    send_sem,
    recv_sem,
):
    me = lax.axis_index("blk")
    rows, features = frames_ref.shape
    width = basis_ref.shape[1]
    span = features // n
    total = n * rows
    others = farthest_first(me, n)

    barrier = pltpu.get_barrier_semaphore()
    for other in others:
        pl.semaphore_signal(
            barrier, inc=1, device_id={"blk": other}, device_id_type=pl.DeviceIdType.MESH
        )

    stage = pltpu.make_async_copy(frames_ref, staged, own_sem.at[0])
    stage.start()
    fetch_basis = pltpu.make_async_copy(basis_ref, basis_vmem, own_sem.at[1])
    fetch_basis.start()
    fetch_density = pltpu.make_async_copy(density_ref, density_vmem, own_sem.at[2])
    fetch_density.start()

    pl.semaphore_wait(barrier, n - 1)

    def send(src, dst, slot, other):
        pltpu.make_async_remote_copy(
            src_ref=src,
            dst_ref=dst,
            send_sem=send_sem.at[slot],
            recv_sem=recv_sem.at[slot],
            device_id={"blk": other},
            device_id_type=pl.DeviceIdType.MESH,
        ).start()

    def wait_all(buffer, sem):
        part = buffer.at[pl.ds(0, n - 1)]
        pltpu.make_async_copy(part, part, sem).wait()

    for index, other in enumerate(others):
        if index == 4:
            stage.wait()
        send(
            (frames_ref if index < 4 else staged).at[:, pl.ds(pl.multiple_of(other * span, span), span)],
            gathered.at[me],
            0,
            other,
        )
    own = pltpu.make_async_copy(
        staged.at[:, pl.ds(pl.multiple_of(me * span, span), span)], gathered.at[me], own_sem.at[3]
    )
    own.start()

    own_frames = staged[...].astype(jnp.float32)
    own_norms = jnp.sum(own_frames * own_frames, axis=1, keepdims=True)
    norm_parts = []
    rest = own_norms
    for _ in range(3):
        norm_parts.append(rest.astype(jnp.bfloat16).astype(jnp.float32))
        rest = rest - norm_parts[-1]

    row_id = lax.broadcasted_iota(jnp.int32, (rows, rows), 0)
    col_id = lax.broadcasted_iota(jnp.int32, (rows, rows), 1)
    fetch_density.wait()
    density_row = density_vmem[...].astype(jnp.float32)
    density_col = jnp.sum(
        jnp.where(row_id == col_id, jnp.broadcast_to(density_row, (rows, rows)), 0.0),
        axis=1,
        keepdims=True,
    )
    fetch_basis.wait()
    own_basis = basis_vmem[...].astype(jnp.float32)
    lane = lax.broadcasted_iota(jnp.int32, (rows, LANES), 1)
    own_wide = jnp.concatenate(
        [own_basis, jnp.broadcast_to(density_col, (rows, LANES - width))], axis=1
    )
    for index, part in enumerate(norm_parts):
        own_wide = jnp.where(lane == width + 1 + index, part, own_wide)
    aux[me] = own_wide.astype(jnp.bfloat16)
    wait_all(gathered, send_sem.at[0])
    for other in others:
        send(aux.at[me], aux.at[me], 1, other)

    eye = lax.broadcasted_iota(jnp.int32, (total, total), 0) == lax.broadcasted_iota(
        jnp.int32, (total, total), 1
    )
    own.wait()
    wait_all(gathered, recv_sem.at[0])
    block = gathered[...].reshape(total, span)
    gram = lax.dot_general(
        block, block, (((1,), (1,)), ((), ())), preferred_element_type=jnp.float32
    )
    partial[...] = gram.reshape(n, rows, total)
    for other in others:
        send(partial.at[other], arrived.at[me], 2, other)
    arrived[me] = partial[me]

    wait_all(aux, recv_sem.at[1])
    wide = aux[...].astype(jnp.float32).reshape(total, LANES)
    density_all = jnp.sum(jnp.where(eye, wide[:, width : width + 1], 0.0), axis=0, keepdims=True)
    norms = sum(wide[:, width + 1 + index : width + 2 + index] for index in range(3))
    norm_sums = own_norms + jnp.sum(jnp.where(eye, norms, 0.0), axis=0, keepdims=True)
    vectors = wide[:, :width]
    twice = jnp.concatenate([vectors, vectors], axis=1).astype(jnp.bfloat16)

    wait_all(arrived, recv_sem.at[2])

    squared_dist = norm_sums - 2.0 * jnp.sum(arrived[...], axis=0)
    weight = (jnp.exp(squared_dist * (-1.0 / features)) * density_all).astype(jnp.bfloat16)
    numer = jnp.dot(weight, twice, preferred_element_type=jnp.float32)
    totals = jnp.sum(weight.astype(jnp.float32), axis=1, keepdims=True)
    own_applied = numer / totals
    high = own_applied.astype(jnp.bfloat16).astype(jnp.float32)
    applied[me] = jnp.where(lane < width, high, own_applied - high).astype(jnp.bfloat16)
    for other in others:
        send(applied.at[me], applied.at[me], 3, other)

    overlap = lax.dot_general(
        own_basis.astype(jnp.bfloat16),
        vectors.astype(jnp.bfloat16),
        (((1,), (1,)), ((), ())),
        preferred_element_type=jnp.float32,
    )
    overlap_high = overlap.astype(jnp.bfloat16).astype(jnp.float32)
    onto = jnp.concatenate(
        [jnp.transpose(wide)[:width], overlap_high, overlap - overlap_high], axis=0
    ).astype(jnp.bfloat16)

    wait_all(aux, send_sem.at[1])
    wait_all(arrived, send_sem.at[2])
    wait_all(applied, recv_sem.at[3])

    products = jnp.dot(
        onto, applied[...].reshape(total, LANES), preferred_element_type=jnp.float32
    )
    products = products[:, :width] + products[:, width : 2 * width]
    coef_ref[...] = products[:width]
    projection = products[width : width + rows] + products[width + rows :]
    residual_ref[...] = (own_applied[:, :width] - projection * (1.0 / total)).astype(jnp.bfloat16)

    wait_all(applied, send_sem.at[3])


def deliver(residual_vmem, coef_vmem, residual_ref, coef_ref, sem):
    copies = [
        pltpu.make_async_copy(coef_vmem, coef_ref, sem.at[0]),
        pltpu.make_async_copy(residual_vmem, residual_ref, sem.at[1]),
    ]
    for copy in copies:
        copy.start()
    for copy in copies:
        copy.wait()


def shards(n, frames, basis, density):
    rows, features = frames.shape
    width = basis.shape[1]
    total = n * rows
    vmem = pl.BlockSpec(memory_space=pltpu.VMEM)
    operands = (frames, basis, density.reshape(1, rows))
    out_shape = (
        jax.ShapeDtypeStruct((rows, width), jnp.bfloat16),
        jax.ShapeDtypeStruct((width, width), jnp.float32),
    )
    results = pl.pallas_call(
        functools.partial(kernel, n),
        out_shape=out_shape,
        in_specs=[pl.BlockSpec(memory_space=pltpu.HBM)] * 3,
        out_specs=(vmem, vmem),
        scratch_shapes=[
            pltpu.VMEM((n, rows, features // n), jnp.bfloat16),
            pltpu.VMEM((n, rows, LANES), jnp.bfloat16),
            pltpu.VMEM((n, rows, total), jnp.float32),
            pltpu.VMEM((n, rows, total), jnp.float32),
            pltpu.VMEM((n, rows, LANES), jnp.bfloat16),
            pltpu.VMEM((rows, width), jnp.bfloat16),
            pltpu.VMEM((1, rows), jnp.bfloat16),
            pltpu.VMEM((rows, features), jnp.bfloat16),
            pltpu.SemaphoreType.DMA((4,)),
            pltpu.SemaphoreType.DMA((4,)),
            pltpu.SemaphoreType.DMA((4,)),
        ],
        compiler_params=pltpu.CompilerParams(
            collective_id=0, has_side_effects=True, vmem_limit_bytes=32 * 1024 * 1024
        ),
        cost_estimate=pl.CostEstimate(
            flops=2 * total * total * (features // n),
            bytes_accessed=2 * rows * features,
            transcendentals=rows * total,
        ),
    )(*(pltpu.with_memory_space_constraint(x, pltpu.HBM) for x in operands))
    return pl.pallas_call(
        deliver,
        out_shape=out_shape,
        in_specs=[vmem, vmem],
        out_specs=(pl.BlockSpec(memory_space=pltpu.HBM),) * 2,
        scratch_shapes=[pltpu.SemaphoreType.DMA((2,))],
        compiler_params=pltpu.CompilerParams(vmem_limit_bytes=1024 * 1024),
    )(*(pltpu.with_memory_space_constraint(x, pltpu.VMEM) for x in results))


def solution(mesh):
    placed = (P(("groups", "blk"), None), P(("groups", "blk"), None), P(("groups", "blk")))
    return jax.shard_map(
        functools.partial(shards, mesh.shape["blk"]),
        mesh=mesh,
        in_specs=placed,
        out_specs=(P(("groups", "blk"), None), P("groups", None)),
        check_vma=False,
    )
```
